1024 devices in a mesh: dp: 64 (over y, x), replica: 16 (over z, core).
Axes of the slice: x: 8, y: 8, z: 8, core: 2. Of those that a mesh axis runs over, the one named last changes fastest.
Arguments:
- user_rows: bfloat16 [16, 1024, 2048], P('replica', 'dp'), may hold values from -6 to 6
- user_row: int32 [16, 1024], P('replica', 'dp'), may hold values from 0 to 1023, as said below
- segment: int32 [16, 64, 256], P('replica', 'dp'), may hold values from 0 to 15, never falling along the last dimension, each value on 1 to 32 neighbouring positions
- cand_feat: bfloat16 [16, 16384, 2048], P('replica', 'dp'), may hold values from -16 to 16
- grad_score: float32 [16, 16384], P('replica', 'dp'), may hold values from -6 to 6
- u_weight: bfloat16 [2048, 256], replicated, may hold values from -0.125 to 0.125
- v_weight: bfloat16 [256, 2048], replicated, may hold values from -0.375 to 0.375
- bias: float32 [2048], replicated, may hold values from -3 to 3
- w_out: bfloat16 [2048], replicated, may hold values from -6 to 6
Outputs:
- user_grad: float32 [16, 1024, 2048], P('replica', 'dp')
- grad_u: float32 [2048, 256], P('dp')
- grad_vt: float32 [2048, 256], P('dp')
- grad_bias: float32 [2048], P('dp')
- grad_out: float32 [2048], P('dp')
The draws below stay inside these ranges and needn't reach their ends.
Inputs may be any that keep to these rules, and one draw needn't show every extreme that they name: `user_row`: in each group every one of the 1024 user rows is named exactly once; row j is held by the device of dp index j // 16. The 16 requests of one device name at most 1 row of any one holder, and some device reaches 1 for some holder in every draw.
All inputs are finite; a program needn't handle non-finite values.
Results may differ from the reference program's by a relative error of at most 0.013.
Values may be sent and summed in bfloat16 or wider, within the bound.
No kernel may reach another device: no remote copies, remote signals or barrier semaphores. Data moves between devices by JAX's collectives and lax.ppermute only.
A program may use at most 64 MiB of HBM per device.

```python
import math
import jax
import jax.numpy as jnp
import numpy as np
from jax import lax

D = 2048
R = 256
REQ_DEV = 16
CAND_DEV = 256
CAP = 1
SEG_MOST = 32
REQ = 1024
ROWS = 16384
ALL_ROWS = 262144
N_DP = 64
N_REPLICA = 16


def permute_rows(key, values):
    return jax.random.permutation(key, values)


def fresh_order(key):
    return jax.random.permutation(key, REQ_DEV)


def route_group(key):
    keys = jax.random.split(key, 6)
    owners_used = REQ_DEV // CAP
    npairs = owners_used // 4
    full_count = owners_used - npairs
    empty_count = N_DP - full_count - 2 * npairs
    order = jax.random.permutation(keys[0], N_DP)
    paired = jax.random.randint(keys[1], (npairs,), 0, CAP + 1).astype(jnp.int32)
    values = jnp.concatenate([jnp.full((full_count,), CAP, jnp.int32), jnp.zeros((empty_count,), jnp.int32), paired, CAP - paired])
    pattern = jnp.zeros((N_DP,), jnp.int32).at[order].set(values)
    host_perm = jax.random.permutation(keys[2], N_DP)
    owner_perm = jax.random.permutation(keys[3], N_DP)
    counts = pattern[(owner_perm[None, :] - host_perm[:, None]) % N_DP]
    upto = jnp.cumsum(counts, axis=1)
    place = jnp.arange(REQ_DEV, dtype=jnp.int32)
    owner = jnp.sum((upto[:, None, :] <= place[None, :, None]).astype(jnp.int32), axis=2)
    in_host = place[None, :] - jnp.take_along_axis(upto - counts, owner, axis=1)
    before = jnp.cumsum(counts, axis=0) - counts
    rank = jnp.take_along_axis(before, owner, axis=1) + in_host
    positions = jax.vmap(fresh_order)(jax.random.split(keys[4], N_DP))
    rows = owner * REQ_DEV + positions[owner, rank]
    shuffled = jax.vmap(permute_rows)(jax.random.split(keys[5], N_DP), rows)
    return shuffled.reshape(-1)


def draw_user_row(key, part):
    key = jax.random.fold_in(key, 7)
    return jax.vmap(route_group)(jax.random.split(key, N_REPLICA)).astype(jnp.int32)


def strengthened(entries, own_key, source, target, parts, factor):
    owner, partner = [(jnp.arange(entries.shape[axis_at]) // (entries.shape[axis_at] // parts)).reshape([-1 if axis == axis_at else 1 for axis in range(entries.ndim)]) for axis_at in (source, target)]
    chosen = jax.random.permutation(own_key, parts)[partner]
    strong = (owner == chosen) | (owner == (partner + parts // 2) % parts)
    return jnp.where(strong, factor * entries, entries)


def level_of(key, dims, cuts, low, high):
    factor_of = 1.0
    for position, blocks in cuts:
        heights = jax.random.uniform(jax.random.fold_in(jax.random.fold_in(key, 6), position), (blocks,), jnp.float32, low / len(cuts), high / len(cuts))
        factor_of = factor_of * jnp.repeat(jnp.exp(heights), dims[position] // blocks).reshape((-1,) + (1,) * (len(dims) - 1 - position))
    return factor_of


def length_profile(number_of, total, limit, slope):
    weights = [(1 << 20) // math.isqrt(grade ** slope) + 1 for grade in range(2, number_of + 1)]
    surplus, holding = total - limit - (number_of - 1), [1] * (number_of - 1)
    while surplus > 0:
        movable = [i for i in range(number_of - 1) if holding[i] < limit]
        whole, budget = sum([weights[i] for i in movable]), surplus
        for i in movable:
            addition = min(limit - holding[i], max(1, budget * weights[i] // whole), surplus)
            holding[i] = holding[i] + addition
            surplus = surplus - addition
    return np.array([limit] + holding)


def uneven_parts(rng, count, total, most, skew):
    if count == 2:
        one = jax.random.randint(rng, (), max(1, total - most), min(most, total - 1) + 1)
        return jnp.stack([one, total - one])
    lengths = jnp.asarray(length_profile(count, total, most, skew), jnp.int32)
    couples = (count - 1) // 2
    source_of, sink = lengths[1:1 + 2 * couples:2], lengths[2:2 + 2 * couples:2]
    margin = jnp.minimum(source_of - 1, most - sink)
    passed = jax.random.randint(jax.random.fold_in(rng, 1), (couples,), 0, 1 << 20) % (margin + 1)
    lengths = lengths.at[1:1 + 2 * couples:2].set(source_of - passed).at[2:2 + 2 * couples:2].set(sink + passed)
    return lengths[jax.random.permutation(jax.random.fold_in(rng, 2), count)]


def normal_values(rng, dims, width, limit, pieces=(), held_as=jnp.bfloat16):
    entries = jax.random.normal(rng, dims, jnp.float32) * width
    if len(pieces) > 0:
        entries = level_of(rng, dims, pieces, -0.22, 0.18) * entries
    return jnp.clip(entries, min=-limit, max=limit).astype(held_as)


def heavy_noise(key, shape, scale, most, cuts, heavy, kind=jnp.bfloat16):
    values = scale * jax.random.normal(key, shape, jnp.float32)
    if cuts:
        values = values * level_of(key, shape, cuts, -0.22, 0.18)
    return jnp.clip(strengthened(values, jax.random.fold_in(key, 3), *heavy), -most, most).astype(kind)


def setup_inputs(seed: int = 0) -> dict:
    seeds = jax.random.split(jax.random.key(seed), 10)
    return {
        "user_rows": normal_values(seeds[0], (N_REPLICA, REQ, D), 1.0, 6.0, ((0, 16), (1, 64))),
        "user_row": draw_user_row(jax.random.fold_in(seeds[9], 71), 0),
        "segment": jax.vmap(lambda own: jnp.searchsorted(jnp.cumsum(uneven_parts(own, REQ_DEV, CAND_DEV, SEG_MOST, 2)), jnp.arange(CAND_DEV), side="right"))(jax.random.split(seeds[2], N_REPLICA * N_DP)).reshape((N_REPLICA, N_DP, CAND_DEV)).astype(jnp.int32),
        "cand_feat": heavy_noise(seeds[3], (N_REPLICA, ROWS, D), 1.0, 16.0, ((0, 16), (1, 64)), (1, 2, 64, 4.0)),
        "grad_score": normal_values(seeds[4], (N_REPLICA, ROWS), 1.0, 6.0, ((0, 16), (1, 64)), jnp.float32),
        "u_weight": normal_values(seeds[5], (D, R), D ** -0.5, 0.125),
        "v_weight": normal_values(seeds[6], (R, D), R ** -0.5, 0.375),
        "bias": normal_values(seeds[7], (D,), 0.5, 3.0, (), jnp.float32),
        "w_out": normal_values(seeds[8], (D,), 1.0, 6.0),
    }


def cross_block(rows_group, wanted, seg, feat, scores, u_weight, v_weight, bias, w_out):
    local_rows = jnp.take(rows_group, wanted, axis=0)
    user_part = jnp.take(local_rows, seg, axis=0)
    x_zero = (feat.astype(jnp.float32) + user_part.astype(jnp.float32)).astype(jnp.bfloat16)
    low = jnp.dot(x_zero, u_weight, preferred_element_type=jnp.float32).astype(jnp.bfloat16)
    scale_vec = jnp.dot(low, v_weight, preferred_element_type=jnp.float32) + bias[None, :]
    x_wide = x_zero.astype(jnp.float32)
    crossed = x_wide * scale_vec + x_wide
    upstream = scores[:, None] * w_out.astype(jnp.float32)[None, :]
    grad_scale = upstream * x_wide
    grad_scale_b = grad_scale.astype(jnp.bfloat16)
    grad_low = jnp.dot(grad_scale_b, v_weight.T, preferred_element_type=jnp.float32).astype(jnp.bfloat16)
    grad_input = upstream * (scale_vec + 1.0) + jnp.dot(grad_low, u_weight.T, preferred_element_type=jnp.float32)
    member = (seg[None, :] == jnp.arange(REQ_DEV, dtype=jnp.int32)[:, None]).astype(jnp.float32)
    request_grad = jnp.dot(member, grad_input, precision=lax.Precision.HIGHEST, preferred_element_type=jnp.float32)
    part_u = jnp.dot(x_zero.T, grad_low, preferred_element_type=jnp.float32)
    part_vt = jnp.dot(grad_scale_b.T, low, preferred_element_type=jnp.float32)
    part_bias = lax.optimization_barrier(jnp.sum(grad_scale, axis=0))
    part_out = jnp.dot(scores[None, :], crossed, precision=lax.Precision.HIGHEST, preferred_element_type=jnp.float32)[0]
    return (request_grad, part_u, part_vt, part_bias, part_out)

def reference(user_rows, user_row, segment, cand_feat, grad_score, u_weight, v_weight, bias, w_out):
    blocks = N_REPLICA * N_DP
    wanted_all = user_row.reshape(blocks, REQ_DEV)
    seg_all = segment.reshape(blocks, CAND_DEV)
    feat_all = cand_feat.reshape(blocks, CAND_DEV, D)
    score_all = grad_score.reshape(blocks, CAND_DEV)
    block_ids = jnp.arange(blocks, dtype=jnp.int32)

    def advance(carry, inputs):
        index, wanted, seg, feat, scores = inputs
        group = lax.dynamic_index_in_dim(user_rows, index // N_DP, 0, keepdims=False)
        result = cross_block(group, wanted, seg, feat, scores, u_weight, v_weight, bias, w_out)
        carry = tuple((total + term for total, term in zip(carry, result[1:])))
        return (carry, result[0])
    start = (jnp.zeros((D, R), jnp.float32), jnp.zeros((D, R), jnp.float32), jnp.zeros((D,), jnp.float32), jnp.zeros((D,), jnp.float32))
    totals, grads_user = lax.scan(advance, start, (block_ids, wanted_all, seg_all, feat_all, score_all))
    group_index = jnp.broadcast_to((block_ids // N_DP)[:, None], (blocks, REQ_DEV))
    user_grad = jnp.zeros((N_REPLICA, REQ_DEV * N_DP, D), jnp.float32).at[group_index, wanted_all].set(grads_user)
    factor = 1.0 / math.sqrt(ALL_ROWS)
    return (user_grad, totals[0] * factor, totals[1] * factor, totals[2] * factor, totals[3] * factor)
```

```python
import functools
import math

import jax
import jax.numpy as jnp
from jax import lax
from jax.experimental import pallas as pl
from jax.experimental.pallas import tpu as pltpu
from jax.sharding import PartitionSpec as P

F32 = jnp.float32
BF16 = jnp.bfloat16
LANES = 128
PIECES = 8
NT = (((1,), (1,)), ((), ()))
TN = (((0,), (0,)), ((), ()))
PARAMS = pltpu.CompilerParams(vmem_limit_bytes=40 << 20)


def dot(a, b, dims=(((1,), (0,)), ((), ()))):
    return lax.dot_general(a, b, dims, preferred_element_type=F32)


def iota(shape, dim):
    return lax.broadcasted_iota(jnp.int32, shape, dim)


def split_in_two(x):
    high = x.astype(BF16)
    return high, (x - high.astype(F32)).astype(BF16)


def as_columns(row):
    return jnp.transpose(jnp.broadcast_to(row, (LANES, row.shape[1])))


def request_kernel(wanted_ref, seg_ref, score_ref, feat_ref, user_ref, slots_ref, swap_ref, wide):
    peers, req = slots_ref.shape[0], wanted_ref.shape[1]
    rows, width = feat_ref.shape
    piece = width // PIECES
    wanted = wanted_ref[...]
    owner = lax.div(wanted, jnp.int32(req))
    local = wanted - owner * req
    scores = score_ref[...]
    to_owner = (iota((peers, req), 0) == owner).astype(BF16)
    place = (iota((LANES, req), 0) == local).astype(BF16)
    mine = iota((req, rows), 0) == seg_ref[...]
    total_high, total_low = split_in_two(
        jnp.sum(jnp.where(mine, scores, 0.0), axis=1, keepdims=True)
    )
    lane = iota((req, LANES), 1)
    totals = jnp.where(
        lane == req,
        total_high.astype(F32),
        jnp.where(lane == req + 1, total_low.astype(F32), 0.0),
    ).astype(BF16)
    extra = dot(to_owner, place, NT) + dot(to_owner, totals)
    weights = jnp.where(mine, scores, 0.0).astype(BF16)
    weights = dot(to_owner, weights).astype(BF16)
    wide[:, :, piece:] = jnp.zeros((peers, PIECES, LANES), F32)
    wide[:, 0, piece:] = extra
    for p in range(PIECES):
        wide[:, p, :piece] = dot(weights, feat_ref[:, p * piece : (p + 1) * piece])
    slots_ref[...] = wide[...].astype(BF16)
    score_high, score_low = split_in_two(scores)
    line = iota((16, rows), 0)
    swap_ref[:rows, :] = feat_ref[...]
    swap_ref[rows : rows + 16, :] = jnp.zeros((16, width), BF16)
    swap_ref[rows : rows + 16, :rows] = jnp.where(
        line == 0,
        score_high.astype(F32),
        jnp.where(line == 1, score_low.astype(F32), 0.0),
    ).astype(BF16)
    swap_ref[rows + 16 :, :] = user_ref[...]


def main_kernel(
    at_ref, feat_ref, score_ref, user_ref, swap_ref, u_ref, v_ref, bias_ref, w_ref,
    grad_ref, half_ref, vw_ref, user_half_ref, tail_ref, both,
):
    dp, core = at_ref[0], at_ref[1]
    rows, width = feat_ref.shape
    rank = v_ref.shape[0]
    part = tail_ref.shape[0]
    w_row = w_ref[...].astype(F32)
    vw = (v_ref[...].astype(F32) * w_row).astype(BF16)
    vw_ref[...] = vw
    half_ref[...] = u_ref[...]

    @pl.when(core == 1)
    def _():
        half_ref[...] = jnp.transpose(vw)

    both[:rows, :] = feat_ref[...]
    both[rows:, :] = swap_ref[:rows, :]
    marks = swap_ref[rows : rows + 16, :rows].astype(F32)
    scores = jnp.concatenate(
        [as_columns(score_ref[...]), as_columns(marks[0:1, :] + marks[1:2, :])], axis=0
    )
    low = dot(both[...], half_ref[...])
    scaled = [
        low[:, k : k + LANES] * scores for k in range(0, rank, LANES)
    ]
    lane = iota((2 * rows, LANES), 1)
    scaled.append(jnp.where(lane < 4, scores, 0.0))
    scaled = jnp.concatenate(scaled, axis=1).astype(BF16)
    grad_ref[...] = dot(both[...], scaled, TN)
    user_half_ref[:16, :] = dot(user_ref[...], half_ref[...])
    user_half_ref[16:, :] = dot(swap_ref[rows + 16 :, :], half_ref[...])
    here = iota((part, width), 1) == dp * part + iota((part, width), 0)
    tail_ref[:, :rank] = dot(here.astype(BF16), v_ref[...], NT)
    lane = iota((part, LANES), 1)
    w_col = jnp.sum(jnp.where(here, w_row, 0.0), axis=1, keepdims=True)
    b_col = jnp.sum(jnp.where(here, bias_ref[...], 0.0), axis=1, keepdims=True)
    tail_ref[:, rank:] = jnp.where(lane == 0, w_col, jnp.where(lane == 1, b_col, 0.0))


def pick_kernel(slots_ref, out_ref, wide):
    req = out_ref.shape[0]
    piece = slots_ref.shape[2] - LANES
    wide[...] = slots_ref[...].astype(F32)
    extra = wide[:, 0, piece:].astype(BF16)
    lane = iota(extra.shape, 1)
    order = jnp.where(lane < req, extra.astype(F32), 0.0).astype(BF16)[:, :req]
    for p in range(PIECES):
        got = wide[:, p, :piece].astype(BF16)
        out_ref[:, p * piece : (p + 1) * piece] = dot(order, got, TN).astype(BF16)
    out_ref[:, PIECES * piece :] = dot(order, extra, TN).astype(BF16)


def total_of(pack, width, req):
    at = width + req
    return pack[:, at : at + 1].astype(F32) + pack[:, at + 1 : at + 2].astype(F32)


def merge_kernel(grad_ref, own_ref, other_ref, user_ref, swap_ref, half_ref, user_half_ref, out_ref):
    req, width = user_ref.shape
    rank = half_ref.shape[1]
    peers = out_ref.shape[0]
    half = half_ref[...]
    lines, factors = [], []
    lane = iota((req, LANES), 1)
    for at, pack_ref, user in (
        (0, own_ref, user_ref[...]),
        (req, other_ref, swap_ref[...]),
    ):
        pack = pack_ref[...]
        sums = pack[:, :width]
        total = total_of(pack, width, req)
        user_half = user_half_ref[at : at + req, :]
        both = dot(sums, half) + total * user_half
        lines += [sums, user]
        factors += [
            jnp.concatenate([user_half, jnp.zeros((req, LANES), F32)], axis=1),
            jnp.concatenate([both, jnp.where(lane < 4, total, 0.0)], axis=1),
        ]
    lines = jnp.concatenate(lines, axis=0)
    factors = jnp.concatenate(factors, axis=0).astype(BF16)
    grad = grad_ref[...] + dot(lines, factors, TN)
    blocks = grad.reshape(peers, 4, 8, rank + LANES)
    lane = iota((peers, 8, LANES), 2)
    sums = jnp.zeros((peers, 8, LANES), F32)
    for q in range(4):
        out_ref[:, :, q * rank : (q + 1) * rank] = blocks[:, q, :, :rank].astype(BF16)
        sums = jnp.where(lane == q, blocks[:, q, :, rank:], sums)
    out_ref[:, :, 4 * rank :] = sums.astype(BF16)


def user_grad_kernel(pack_ref, user_ref, u_ref, v_ref, vw_ref, bias_ref, w_ref, out_ref):
    req, width = user_ref.shape
    pack = pack_ref[...]
    sums = pack[:, :width]
    total = total_of(pack, width, req)
    user = user_ref[...]
    u, vw = u_ref[...], vw_ref[...]
    low = dot(sums, u) + total * dot(user, u)
    grad_low = dot(sums, vw, NT) + total * dot(user, vw, NT)
    w_row = w_ref[...].astype(F32)
    out_ref[...] = (
        w_row * (dot(low.astype(BF16), v_ref[...]) + total * (bias_ref[...] + 1.0))
        + dot(grad_low.astype(BF16), u, NT)
    )


def sum_kernel(in_ref, out_ref):
    total = jnp.sum(in_ref[...].astype(F32), axis=0).astype(BF16)
    out_ref[...] = jnp.broadcast_to(total[None], out_ref.shape)


def last_kernel(factor, in_ref, tail_ref, grad_u_ref, grad_vt_ref, bias_ref, out_ref):
    part, rank = grad_u_ref.shape
    replicas = in_ref.shape[0]
    sums = [
        sum(in_ref[k].astype(F32) for k in range(core, replicas, 2)) * factor for core in (0, 1)
    ]
    low, grad_low = (
        jnp.concatenate([s[:, q * rank : (q + 1) * rank] for q in range(4)], axis=0) for s in sums
    )
    column = jnp.concatenate(
        [sums[0][:, 4 * rank + q : 4 * rank + q + 1] for q in range(4)], axis=0
    )
    tail = tail_ref[...]
    w_col, b_col = tail[:, rank : rank + 1], tail[:, rank + 1 : rank + 2]
    grad_u_ref[...] = grad_low
    grad_vt_ref[...] = w_col * low
    out_col = jnp.sum(tail[:, :rank] * low, axis=1, keepdims=True) + (b_col + 1.0) * column
    bias_ref[...] = jnp.transpose(jnp.broadcast_to(w_col * column, (part, LANES)))[0:1, :]
    out_ref[...] = jnp.transpose(jnp.broadcast_to(out_col, (part, LANES)))[0:1, :]


def call(kernel, out, *args, scratch=(), scalars=0):
    specs = [pl.BlockSpec(memory_space=pltpu.SMEM)] * scalars
    specs += [pl.BlockSpec(memory_space=pltpu.VMEM)] * (len(args) - scalars)
    return pl.pallas_call(
        kernel,
        out_shape=out,
        in_specs=specs,
        out_specs=jax.tree.map(lambda _: pl.BlockSpec(memory_space=pltpu.VMEM), out),
        scratch_shapes=list(scratch),
        compiler_params=PARAMS,
    )(*args)


def per_device(
    user_rows, user_row, segment, cand_feat, grad_score, u_weight, v_weight, bias, w_out
):
    user, feat, seg = user_rows[0], cand_feat[0], segment[0]
    peers, replicas = lax.axis_size("dp"), lax.axis_size("replica")
    req, width = user.shape
    rows = feat.shape[0]
    rank = u_weight.shape[1]
    part = width // peers
    piece = width // PIECES
    shape = jax.ShapeDtypeStruct
    bias, w_out = bias[None], w_out[None]
    pairs = [(i, i ^ 1) for i in range(replicas)]
    at = jnp.stack([lax.axis_index("dp"), lax.axis_index("replica") % 2]).astype(jnp.int32)

    slots, swap = call(
        request_kernel,
        (
            shape((peers, PIECES, piece + LANES), BF16),
            shape((rows + 16 + req, width), BF16),
        ),
        user_row, seg, grad_score, feat, user,
        scratch=[pltpu.VMEM((peers, PIECES, piece + LANES), F32)],
    )
    arrived = lax.all_to_all(slots, "dp", split_axis=0, concat_axis=0, tiled=True)
    swapped = lax.ppermute(swap, "replica", pairs)
    grad, half, vw, user_half, tail = call(
        main_kernel,
        (
            shape((width, rank + LANES), F32),
            shape((width, rank), BF16),
            shape((rank, width), BF16),
            shape((2 * req, rank), F32),
            shape((part, rank + LANES), F32),
        ),
        at, feat, grad_score, user, swapped, u_weight, v_weight, bias, w_out,
        scratch=[pltpu.VMEM((2 * rows, width), BF16)],
        scalars=1,
    )
    own = call(
        pick_kernel,
        shape((req, width + LANES), BF16),
        arrived,
        scratch=[pltpu.VMEM((peers, PIECES, piece + LANES), F32)],
    )
    other = lax.ppermute(own, "replica", pairs)
    parts = call(
        merge_kernel,
        shape((peers, 8, 4 * rank + LANES), BF16),
        grad, own, other, user, swapped[rows + 16 :], half, user_half,
    )
    received = lax.all_to_all(parts, "dp", split_axis=0, concat_axis=0, tiled=True)
    user_grad = call(
        user_grad_kernel,
        shape((req, width), F32),
        own, user, u_weight, v_weight, vw, bias, w_out,
    )
    copies = call(sum_kernel, shape((replicas, 8, 4 * rank + LANES), BF16), received)
    gathered = lax.all_to_all(copies, "replica", split_axis=0, concat_axis=0, tiled=True)
    factor = 1.0 / math.sqrt(rows * peers * replicas)
    grad_u, grad_vt, grad_bias, grad_out = call(
        functools.partial(last_kernel, factor),
        (
            shape((part, rank), F32),
            shape((part, rank), F32),
            shape((1, part), F32),
            shape((1, part), F32),
        ),
        gathered, tail,
    )
    return (user_grad[None], grad_u, grad_vt, grad_bias[0], grad_out[0])


def solution(mesh):
    placed = (
        P("replica", "dp", None),
        P("replica", "dp"),
        P("replica", "dp", None),
        P("replica", "dp", None),
        P("replica", "dp"),
        P(),
        P(),
        P(),
        P(),
    )
    return jax.shard_map(
        per_device,
        mesh=mesh,
        in_specs=placed,
        out_specs=(P("replica", "dp", None), P("dp", None), P("dp", None), P("dp"), P("dp")),
        check_vma=False,
    )
```

```python
import functools
import math

import jax
import jax.numpy as jnp
from jax import lax
from jax.experimental import pallas as pl
from jax.experimental.pallas import tpu as pltpu
from jax.sharding import PartitionSpec as P

F32 = jnp.float32
BF16 = jnp.bfloat16
LANES = 128
PIECES = 2
NT = (((1,), (1,)), ((), ()))
TN = (((0,), (0,)), ((), ()))


def dot(a, b, dims=(((1,), (0,)), ((), ()))):
    return lax.dot_general(a, b, dims, preferred_element_type=F32)


def iota(shape, dim):
    return lax.broadcasted_iota(jnp.int32, shape, dim)


def split_in_two(x):
    high = x.astype(BF16)
    return high, (x - high.astype(F32)).astype(BF16)


def as_columns(row):
    return jnp.transpose(jnp.broadcast_to(row, (LANES, row.shape[1])))


def request_kernel(wait, wanted_ref, seg_ref, score_ref, feat_ref, slots_ref, wide):
    peers, req = slots_ref.shape[0], wanted_ref.shape[1]
    rows, width = feat_ref.shape
    piece = width // PIECES
    wait(0, 1, 2)
    wanted = wanted_ref[...]
    owner = lax.div(wanted, jnp.int32(req))
    local = wanted - owner * req
    scores = score_ref[...]
    to_owner = (iota((peers, req), 0) == owner).astype(BF16)
    place = (iota((LANES, req), 0) == local).astype(BF16)
    mine = iota((req, rows), 0) == seg_ref[...]
    total_high, total_low = split_in_two(
        jnp.sum(jnp.where(mine, scores, 0.0), axis=1, keepdims=True)
    )
    lane = iota((req, LANES), 1)
    totals = jnp.where(
        lane == req,
        total_high.astype(F32),
        jnp.where(lane == req + 1, total_low.astype(F32), 0.0),
    ).astype(BF16)
    extra = dot(to_owner, place, NT) + dot(to_owner, totals)
    weights = jnp.where(mine, scores, 0.0).astype(BF16)
    weights = dot(to_owner, weights).astype(BF16)
    wide[:, 0, piece:] = extra
    for p in range(1, PIECES):
        wide[:, p, piece:] = jnp.zeros((peers, LANES), F32)
    wait(3)
    for p in range(PIECES):
        wide[:, p, :piece] = dot(weights, feat_ref[:, p * piece : (p + 1) * piece])
    slots_ref[...] = wide[...].astype(BF16)


def swap_kernel(wait, slots_any, feat_ref, score_ref, user_ref, swap_ref):
    wait(1, 2, 3)
    rows, width = feat_ref.shape
    score_high, score_low = split_in_two(score_ref[...])
    line = iota((16, rows), 0)
    swap_ref[:rows, :] = feat_ref[...]
    swap_ref[rows : rows + 16, :] = jnp.zeros((16, width), BF16)
    swap_ref[rows : rows + 16, :rows] = jnp.where(
        line == 0,
        score_high.astype(F32),
        jnp.where(line == 1, score_low.astype(F32), 0.0),
    ).astype(BF16)
    swap_ref[rows + 16 :, :] = user_ref[...]


def lay_out(grad, out_ref, base, base_sums):
    peers, rank = out_ref.shape[0], grad.shape[1] - LANES
    blocks = grad.reshape(peers, 4, 8, rank + LANES)
    lane = iota((peers, 8, LANES), 2)
    sums = jnp.zeros((peers, 8, LANES), F32)
    for q in range(4):
        out_ref[:, :, q * rank : (q + 1) * rank] = (blocks[:, q, :, :rank] + base(q)).astype(BF16)
        sums = jnp.where(lane == q, blocks[:, q, :, rank:], sums)
    out_ref[:, :, 4 * rank :] = (sums + base_sums).astype(BF16)


def main_kernel(
    wait, at_ref, feat_ref, score_ref, user_ref, swap_ref, u_ref, v_ref, bias_ref, w_ref,
    base_ref, half_ref, vw_ref, users_ref, user_half_ref, tail_ref, both,
):
    wait(*range(1, 9))
    dp, core = at_ref[0], at_ref[1]
    rows, width = feat_ref.shape
    rank = v_ref.shape[0]
    part = tail_ref.shape[0]
    w_row = w_ref[...].astype(F32)
    vw = (v_ref[...].astype(F32) * w_row).astype(BF16)
    vw_ref[...] = vw
    half_ref[...] = u_ref[...]

    @pl.when(core == 1)
    def _():
        half_ref[...] = jnp.transpose(vw)

    both[:rows, :] = feat_ref[...]
    both[rows:, :] = swap_ref[:rows, :]
    marks = swap_ref[rows : rows + 16, :rows].astype(F32)
    scores = jnp.concatenate(
        [as_columns(score_ref[...]), as_columns(marks[0:1, :] + marks[1:2, :])], axis=0
    )
    low = dot(both[...], half_ref[...])
    scaled = [
        low[:, k : k + LANES] * scores for k in range(0, rank, LANES)
    ]
    lane = iota((2 * rows, LANES), 1)
    scaled.append(jnp.where(lane < 4, scores, 0.0))
    scaled = jnp.concatenate(scaled, axis=1).astype(BF16)
    lay_out(dot(both[...], scaled, TN), base_ref, lambda q: 0.0, 0.0)
    users_ref[:16, :] = user_ref[...]
    users_ref[16:, :] = swap_ref[rows + 16 :, :]
    user_half_ref[...] = dot(users_ref[...], half_ref[...])
    here = iota((part, width), 1) == dp * part + iota((part, width), 0)
    tail_ref[:, :rank] = dot(here.astype(BF16), v_ref[...], NT)
    lane = iota((part, LANES), 1)
    w_col = jnp.sum(jnp.where(here, w_row, 0.0), axis=1, keepdims=True)
    b_col = jnp.sum(jnp.where(here, bias_ref[...], 0.0), axis=1, keepdims=True)
    tail_ref[:, rank:] = jnp.where(lane == 0, w_col, jnp.where(lane == 1, b_col, 0.0))


def pick_kernel(wait, slots_ref, tail_any, out_ref, wide):
    req = out_ref.shape[0]
    piece = slots_ref.shape[2] - LANES
    wide[...] = slots_ref[...].astype(F32)
    extra = wide[:, 0, piece:].astype(BF16)
    lane = iota(extra.shape, 1)
    order = jnp.where(lane < req, extra.astype(F32), 0.0).astype(BF16)[:, :req]
    for p in range(PIECES):
        got = wide[:, p, :piece].astype(BF16)
        out_ref[:, p * piece : (p + 1) * piece] = dot(order, got, TN).astype(BF16)
    out_ref[:, PIECES * piece :] = dot(order, extra, TN).astype(BF16)


def total_of(pack, width, req):
    at = width + req
    return pack[:, at : at + 1].astype(F32) + pack[:, at + 1 : at + 2].astype(F32)


def merge_kernel(wait, base_ref, own_ref, other_ref, users_ref, half_ref, user_half_ref, out_ref):
    req, width = users_ref.shape[0] // 2, users_ref.shape[1]
    rank = half_ref.shape[1]
    wait(3, 4, 5)
    half = half_ref[...]
    lines, factors = [], []
    lane = iota((req, LANES), 1)
    for at, pack_ref, user in (
        (0, own_ref, users_ref[:req, :]),
        (req, other_ref, users_ref[req:, :]),
    ):
        pack = pack_ref[...]
        sums = pack[:, :width]
        total = total_of(pack, width, req)
        user_half = user_half_ref[at : at + req, :]
        both = dot(sums, half) + total * user_half
        lines += [sums, user]
        factors += [
            jnp.concatenate([user_half, jnp.zeros((req, LANES), F32)], axis=1),
            jnp.concatenate([both, jnp.where(lane < 4, total, 0.0)], axis=1),
        ]
    lines = jnp.concatenate(lines, axis=0)
    factors = jnp.concatenate(factors, axis=0).astype(BF16)
    wait(0)
    lay_out(
        dot(lines, factors, TN),
        out_ref,
        lambda q: base_ref[:, :, q * rank : (q + 1) * rank].astype(F32),
        base_ref[:, :, 4 * rank :].astype(F32),
    )


def user_grad_kernel(wait, pack_ref, user_ref, u_ref, v_ref, vw_ref, bias_ref, w_ref, out_ref):
    wait(*range(1, 7))
    req, width = user_ref.shape
    pack = pack_ref[...]
    sums = pack[:, :width]
    total = total_of(pack, width, req)
    user = user_ref[...]
    u, vw = u_ref[...], vw_ref[...]
    low = dot(sums, u) + total * dot(user, u)
    grad_low = dot(sums, vw, NT) + total * dot(user, vw, NT)
    w_row = w_ref[...].astype(F32)
    out_ref[...] = (
        w_row * (dot(low.astype(BF16), v_ref[...]) + total * (bias_ref[...] + 1.0))
        + dot(grad_low.astype(BF16), u, NT)
    )


def sum_kernel(wait, in_ref, out_ref):
    total = jnp.sum(in_ref[...].astype(F32), axis=0).astype(BF16)
    out_ref[...] = jnp.broadcast_to(total[None], out_ref.shape)


def last_kernel(factor, wait, in_ref, tail_ref, grad_u_ref, grad_vt_ref, bias_ref, out_ref):
    wait(1)
    part, rank = grad_u_ref.shape
    replicas = in_ref.shape[0]
    sums = [
        sum(in_ref[k].astype(F32) for k in range(core, replicas, 2)) * factor for core in (0, 1)
    ]
    low, grad_low = (
        jnp.concatenate([s[:, q * rank : (q + 1) * rank] for q in range(4)], axis=0) for s in sums
    )
    column = jnp.concatenate(
        [sums[0][:, 4 * rank + q : 4 * rank + q + 1] for q in range(4)], axis=0
    )
    tail = tail_ref[...]
    w_col, b_col = tail[:, rank : rank + 1], tail[:, rank + 1 : rank + 2]
    grad_u_ref[...] = grad_low
    grad_vt_ref[...] = w_col * low
    out_col = jnp.sum(tail[:, :rank] * low, axis=1, keepdims=True) + (b_col + 1.0) * column
    bias_ref[...] = jnp.transpose(jnp.broadcast_to(w_col * column, (part, LANES)))[0:1, :]
    out_ref[...] = jnp.transpose(jnp.broadcast_to(out_col, (part, LANES)))[0:1, :]


def call(kernel, out, *args, places="", out_places="", scratch=(), room=24, cost=None):
    spaces = {"s": pltpu.SMEM, "a": pl.ANY, "h": pltpu.HBM, "n": pl.ANY, "-": pltpu.VMEM}
    several = isinstance(out, tuple)
    outs = out if several else (out,)
    places = places + "-" * (len(args) - len(places))
    out_places = out_places + "-" * (len(outs) - len(out_places))
    staged = [k for k, place in enumerate(places) if place in "hn"]
    late = [k for k, place in enumerate(out_places) if place in "hn"]
    args = [
        pltpu.with_memory_space_constraint(arg, pltpu.HBM) if place == "h" else arg
        for arg, place in zip(args, places)
    ]
    n_in, n_out, n_scratch = len(args), len(outs), len(scratch)

    def body(*refs):
        refs = list(refs)
        ins, results = refs[:n_in], refs[n_in : n_in + n_out]
        rest = refs[n_in + n_out :]
        own, rest = rest[:n_scratch], rest[n_scratch:]
        buffers, rest = rest[: len(staged)], rest[len(staged) :]
        out_buffers, rest = rest[: len(late)], rest[len(late) :]
        copies = {}
        for at, k in enumerate(staged):
            copies[k] = pltpu.make_async_copy(ins[k], buffers[at], rest[0].at[at])
            copies[k].start()
            ins[k] = buffers[at]
        targets = {}
        for at, k in enumerate(late):
            targets[k] = results[k]
            results[k] = out_buffers[at]

        def wait(*which):
            for k in which:
                copies.pop(k).wait()

        kernel(wait, *ins, *results, *own)
        assert not copies
        ends = [
            pltpu.make_async_copy(results[k], targets[k], rest[-1].at[at])
            for at, k in enumerate(late)
        ]
        for copy in ends:
            copy.start()
        for copy in ends:
            copy.wait()

    def like(x):
        return pltpu.VMEM(x.shape, x.dtype)

    extra = [like(args[k]) for k in staged] + [like(outs[k]) for k in late]
    extra += [pltpu.SemaphoreType.DMA((len(group),)) for group in (staged, late) if group]
    out_specs = tuple(pl.BlockSpec(memory_space=spaces[place]) for place in out_places)
    pinned = tuple(
        pltpu.HBM(x.shape, x.dtype) if place == "h" else x for x, place in zip(outs, out_places)
    )
    return pl.pallas_call(
        body,
        out_shape=pinned if several else pinned[0],
        in_specs=[pl.BlockSpec(memory_space=spaces[place]) for place in places],
        out_specs=out_specs if several else out_specs[0],
        scratch_shapes=list(scratch) + extra,
        compiler_params=pltpu.CompilerParams(vmem_limit_bytes=room << 20),
        cost_estimate=cost,
    )(*args)


def per_device(
    user_rows, user_row, segment, cand_feat, grad_score, u_weight, v_weight, bias, w_out
):
    user, feat, seg = user_rows[0], cand_feat[0], segment[0]
    peers, replicas = lax.axis_size("dp"), lax.axis_size("replica")
    req, width = user.shape
    rows = feat.shape[0]
    rank = u_weight.shape[1]
    part = width // peers
    piece = width // PIECES
    shape = jax.ShapeDtypeStruct
    bias, w_out = bias[None], w_out[None]
    pairs = [(i, i ^ 1) for i in range(replicas)]
    at = jnp.stack([lax.axis_index("dp"), lax.axis_index("replica") % 2]).astype(jnp.int32)

    message = (peers, PIECES, piece + LANES)
    slots = call(
        request_kernel,
        shape(message, BF16),
        user_row, seg, grad_score, feat,
        places="hhhh",
        scratch=[pltpu.VMEM(message, F32)],
    )
    swap = call(
        swap_kernel,
        shape((rows + 16 + req, width), BF16),
        slots, feat, grad_score, user,
        places="ahhh",
    )
    arrived = lax.all_to_all(slots, "dp", split_axis=0, concat_axis=0, tiled=True)
    swapped = lax.ppermute(swap, "replica", pairs)
    base, half, vw, users, user_half, tail = call(
        main_kernel,
        (
            shape((peers, 8, 4 * rank + LANES), BF16),
            shape((width, rank), BF16),
            shape((rank, width), BF16),
            shape((2 * req, width), BF16),
            shape((2 * req, rank), F32),
            shape((part, rank + LANES), F32),
        ),
        at, feat, grad_score, user, swapped, u_weight, v_weight, bias, w_out,
        scratch=[pltpu.VMEM((2 * rows, width), BF16)],
        places="shhhnhhhh",
        out_places="nhhnnn",
        cost=pl.CostEstimate(flops=1, bytes_accessed=1, transcendentals=0),
    )
    own = call(
        pick_kernel,
        shape((req, width + LANES), BF16),
        arrived, tail,
        places="-a",
        scratch=[pltpu.VMEM(message, F32)],
    )
    other = lax.ppermute(own, "replica", pairs)
    parts = call(
        merge_kernel,
        shape((peers, 8, 4 * rank + LANES), BF16),
        base, own, other, users, half, user_half,
        places="n--nnn",
    )
    received = lax.all_to_all(parts, "dp", split_axis=0, concat_axis=0, tiled=True)
    user_grad = call(
        user_grad_kernel,
        shape((req, width), F32),
        own, user, u_weight, v_weight, vw, bias, w_out,
        places="-hhhnhh",
    )
    copies = call(sum_kernel, shape((replicas, 8, 4 * rank + LANES), BF16), received)
    gathered = lax.all_to_all(copies, "replica", split_axis=0, concat_axis=0, tiled=True)
    factor = 1.0 / math.sqrt(rows * peers * replicas)
    grad_u, grad_vt, grad_bias, grad_out = call(
        functools.partial(last_kernel, factor),
        (
            shape((part, rank), F32),
            shape((part, rank), F32),
            shape((1, part), F32),
            shape((1, part), F32),
        ),
        gathered, tail,
        places="-n",
    )
    return (user_grad[None], grad_u, grad_vt, grad_bias[0], grad_out[0])


def solution(mesh):
    placed = (
        P("replica", "dp", None),
        P("replica", "dp"),
        P("replica", "dp", None),
        P("replica", "dp", None),
        P("replica", "dp"),
        P(),
        P(),
        P(),
        P(),
    )
    return jax.shard_map(
        per_device,
        mesh=mesh,
        in_specs=placed,
        out_specs=(P("replica", "dp", None), P("dp", None), P("dp", None), P("dp"), P("dp")),
        check_vma=False,
    )
```

```python
import functools
import math

import jax
import jax.numpy as jnp
from jax import lax
from jax.experimental import pallas as pl
from jax.experimental.pallas import tpu as pltpu
from jax.sharding import PartitionSpec as P

F32 = jnp.float32
BF16 = jnp.bfloat16
LANES = 128
PIECES = 2
NT = (((1,), (1,)), ((), ()))
TN = (((0,), (0,)), ((), ()))


def dot(a, b, dims=(((1,), (0,)), ((), ()))):
    return lax.dot_general(a, b, dims, preferred_element_type=F32)


def iota(shape, dim):
    return lax.broadcasted_iota(jnp.int32, shape, dim)


def split_in_two(x):
    high = x.astype(BF16)
    return high, (x - high.astype(F32)).astype(BF16)


def as_columns(row):
    return jnp.transpose(jnp.broadcast_to(row, (LANES, row.shape[1])))


def request_kernel(wait, wanted_ref, seg_ref, score_ref, feat_ref, slots_ref, wide):
    peers, req = slots_ref.shape[0], wanted_ref.shape[1]
    rows, width = feat_ref.shape
    piece = width // PIECES
    wait(0, 1, 2)
    wanted = wanted_ref[...]
    owner = lax.div(wanted, jnp.int32(req))
    local = wanted - owner * req
    scores = score_ref[...]
    to_owner = (iota((peers, req), 0) == owner).astype(BF16)
    place = (iota((LANES, req), 0) == local).astype(BF16)
    mine = iota((req, rows), 0) == seg_ref[...]
    total_high, total_low = split_in_two(
        jnp.sum(jnp.where(mine, scores, 0.0), axis=1, keepdims=True)
    )
    lane = iota((req, LANES), 1)
    totals = jnp.where(
        lane == req,
        total_high.astype(F32),
        jnp.where(lane == req + 1, total_low.astype(F32), 0.0),
    ).astype(BF16)
    extra = dot(to_owner, place, NT) + dot(to_owner, totals)
    weights = jnp.where(mine, scores, 0.0).astype(BF16)
    weights = dot(to_owner, weights).astype(BF16)
    wide[:, 0, piece:] = extra
    for p in range(1, PIECES):
        wide[:, p, piece:] = jnp.zeros((peers, LANES), F32)
    wait(3)
    for p in range(PIECES):
        wide[:, p, :piece] = dot(weights, feat_ref[:, p * piece : (p + 1) * piece])
    slots_ref[...] = wide[...].astype(BF16)


def swap_kernel(wait, slots_any, score_ref, user_ref, swap_ref):
    wait(1, 2)
    rows, width = score_ref.shape[1], user_ref.shape[1]
    score_high, score_low = split_in_two(score_ref[...])
    line = iota((16, rows), 0)
    swap_ref[:16, :] = jnp.zeros((16, width), BF16)
    swap_ref[:16, :rows] = jnp.where(
        line == 0,
        score_high.astype(F32),
        jnp.where(line == 1, score_low.astype(F32), 0.0),
    ).astype(BF16)
    swap_ref[16:, :] = user_ref[...]


def lay_out(grad, out_ref, base, base_sums):
    peers, rank = out_ref.shape[0], grad.shape[1] - LANES
    blocks = grad.reshape(peers, 4, 8, rank + LANES)
    lane = iota((peers, 8, LANES), 2)
    sums = jnp.zeros((peers, 8, LANES), F32)
    for q in range(4):
        out_ref[:, :, q * rank : (q + 1) * rank] = (blocks[:, q, :, :rank] + base(q)).astype(BF16)
        sums = jnp.where(lane == q, blocks[:, q, :, rank:], sums)
    out_ref[:, :, 4 * rank :] = (sums + base_sums).astype(BF16)


def main_kernel(
    wait, at_ref, feat_ref, score_ref, user_ref, other_ref, swap_ref, u_ref, v_ref, bias_ref, w_ref,
    base_ref, half_ref, vw_ref, users_ref, user_half_ref, tail_ref, both,
):
    wait(*range(1, 10))
    dp, core = at_ref[0], at_ref[1]
    rows, width = feat_ref.shape
    rank = v_ref.shape[0]
    part = tail_ref.shape[0]
    w_row = w_ref[...].astype(F32)
    vw = (v_ref[...].astype(F32) * w_row).astype(BF16)
    vw_ref[...] = vw
    half_ref[...] = u_ref[...]

    @pl.when(core == 1)
    def _():
        half_ref[...] = jnp.transpose(vw)

    both[:rows, :] = feat_ref[...]
    both[rows:, :] = other_ref[...]
    marks = swap_ref[:16, :rows].astype(F32)
    scores = jnp.concatenate(
        [as_columns(score_ref[...]), as_columns(marks[0:1, :] + marks[1:2, :])], axis=0
    )
    low = dot(both[...], half_ref[...])
    scaled = [
        low[:, k : k + LANES] * scores for k in range(0, rank, LANES)
    ]
    lane = iota((2 * rows, LANES), 1)
    scaled.append(jnp.where(lane < 4, scores, 0.0))
    scaled = jnp.concatenate(scaled, axis=1).astype(BF16)
    lay_out(dot(both[...], scaled, TN), base_ref, lambda q: 0.0, 0.0)
    users_ref[:16, :] = user_ref[...]
    users_ref[16:, :] = swap_ref[16:, :]
    user_half_ref[...] = dot(users_ref[...], half_ref[...])
    here = iota((part, width), 1) == dp * part + iota((part, width), 0)
    tail_ref[:, :rank] = dot(here.astype(BF16), v_ref[...], NT)
    lane = iota((part, LANES), 1)
    w_col = jnp.sum(jnp.where(here, w_row, 0.0), axis=1, keepdims=True)
    b_col = jnp.sum(jnp.where(here, bias_ref[...], 0.0), axis=1, keepdims=True)
    tail_ref[:, rank:] = jnp.where(lane == 0, w_col, jnp.where(lane == 1, b_col, 0.0))


def pick_kernel(wait, slots_ref, tail_any, out_ref, wide):
    req = out_ref.shape[0]
    piece = slots_ref.shape[2] - LANES
    wide[...] = slots_ref[...].astype(F32)
    extra = wide[:, 0, piece:].astype(BF16)
    lane = iota(extra.shape, 1)
    order = jnp.where(lane < req, extra.astype(F32), 0.0).astype(BF16)[:, :req]
    for p in range(PIECES):
        got = wide[:, p, :piece].astype(BF16)
        out_ref[:, p * piece : (p + 1) * piece] = dot(order, got, TN).astype(BF16)
    out_ref[:, PIECES * piece :] = dot(order, extra, TN).astype(BF16)


def total_of(pack, width, req):
    at = width + req
    return pack[:, at : at + 1].astype(F32) + pack[:, at + 1 : at + 2].astype(F32)


def merge_kernel(wait, base_ref, own_ref, other_ref, users_ref, half_ref, user_half_ref, out_ref):
    req, width = users_ref.shape[0] // 2, users_ref.shape[1]
    rank = half_ref.shape[1]
    wait(3, 4, 5)
    half = half_ref[...]
    lines, factors = [], []
    lane = iota((req, LANES), 1)
    for at, pack_ref, user in (
        (0, own_ref, users_ref[:req, :]),
        (req, other_ref, users_ref[req:, :]),
    ):
        pack = pack_ref[...]
        sums = pack[:, :width]
        total = total_of(pack, width, req)
        user_half = user_half_ref[at : at + req, :]
        both = dot(sums, half) + total * user_half
        lines += [sums, user]
        factors += [
            jnp.concatenate([user_half, jnp.zeros((req, LANES), F32)], axis=1),
            jnp.concatenate([both, jnp.where(lane < 4, total, 0.0)], axis=1),
        ]
    lines = jnp.concatenate(lines, axis=0)
    factors = jnp.concatenate(factors, axis=0).astype(BF16)
    wait(0)
    lay_out(
        dot(lines, factors, TN),
        out_ref,
        lambda q: base_ref[:, :, q * rank : (q + 1) * rank].astype(F32),
        base_ref[:, :, 4 * rank :].astype(F32),
    )


def user_grad_kernel(wait, pack_ref, user_ref, u_ref, v_ref, vw_ref, bias_ref, w_ref, out_ref):
    wait(*range(1, 7))
    req, width = user_ref.shape
    pack = pack_ref[...]
    sums = pack[:, :width]
    total = total_of(pack, width, req)
    user = user_ref[...]
    u, vw = u_ref[...], vw_ref[...]
    low = dot(sums, u) + total * dot(user, u)
    grad_low = dot(sums, vw, NT) + total * dot(user, vw, NT)
    w_row = w_ref[...].astype(F32)
    out_ref[...] = (
        w_row * (dot(low.astype(BF16), v_ref[...]) + total * (bias_ref[...] + 1.0))
        + dot(grad_low.astype(BF16), u, NT)
    )


def sum_kernel(wait, in_ref, out_ref):
    total = jnp.sum(in_ref[...].astype(F32), axis=0).astype(BF16)
    out_ref[...] = jnp.broadcast_to(total[None], out_ref.shape)


def last_kernel(factor, wait, in_ref, tail_ref, grad_u_ref, grad_vt_ref, bias_ref, out_ref):
    wait(1)
    part, rank = grad_u_ref.shape
    replicas = in_ref.shape[0]
    sums = [
        sum(in_ref[k].astype(F32) for k in range(core, replicas, 2)) * factor for core in (0, 1)
    ]
    low, grad_low = (
        jnp.concatenate([s[:, q * rank : (q + 1) * rank] for q in range(4)], axis=0) for s in sums
    )
    column = jnp.concatenate(
        [sums[0][:, 4 * rank + q : 4 * rank + q + 1] for q in range(4)], axis=0
    )
    tail = tail_ref[...]
    w_col, b_col = tail[:, rank : rank + 1], tail[:, rank + 1 : rank + 2]
    grad_u_ref[...] = grad_low
    grad_vt_ref[...] = w_col * low
    out_col = jnp.sum(tail[:, :rank] * low, axis=1, keepdims=True) + (b_col + 1.0) * column
    bias_ref[...] = jnp.transpose(jnp.broadcast_to(w_col * column, (part, LANES)))[0:1, :]
    out_ref[...] = jnp.transpose(jnp.broadcast_to(out_col, (part, LANES)))[0:1, :]


def call(kernel, out, *args, places="", out_places="", scratch=(), room=24, cost=None):
    spaces = {"s": pltpu.SMEM, "a": pl.ANY, "h": pltpu.HBM, "n": pl.ANY, "-": pltpu.VMEM}
    several = isinstance(out, tuple)
    outs = out if several else (out,)
    places = places + "-" * (len(args) - len(places))
    out_places = out_places + "-" * (len(outs) - len(out_places))
    staged = [k for k, place in enumerate(places) if place in "hn"]
    late = [k for k, place in enumerate(out_places) if place in "hn"]
    args = [
        pltpu.with_memory_space_constraint(arg, pltpu.HBM) if place == "h" else arg
        for arg, place in zip(args, places)
    ]
    n_in, n_out, n_scratch = len(args), len(outs), len(scratch)

    def body(*refs):
        refs = list(refs)
        ins, results = refs[:n_in], refs[n_in : n_in + n_out]
        rest = refs[n_in + n_out :]
        own, rest = rest[:n_scratch], rest[n_scratch:]
        buffers, rest = rest[: len(staged)], rest[len(staged) :]
        out_buffers, rest = rest[: len(late)], rest[len(late) :]
        copies = {}
        for at, k in enumerate(staged):
            copies[k] = pltpu.make_async_copy(ins[k], buffers[at], rest[0].at[at])
            copies[k].start()
            ins[k] = buffers[at]
        targets = {}
        for at, k in enumerate(late):
            targets[k] = results[k]
            results[k] = out_buffers[at]

        def wait(*which):
            for k in which:
                copies.pop(k).wait()

        kernel(wait, *ins, *results, *own)
        assert not copies
        ends = [
            pltpu.make_async_copy(results[k], targets[k], rest[-1].at[at])
            for at, k in enumerate(late)
        ]
        for copy in ends:
            copy.start()
        for copy in ends:
            copy.wait()

    def like(x):
        return pltpu.VMEM(x.shape, x.dtype)

    extra = [like(args[k]) for k in staged] + [like(outs[k]) for k in late]
    extra += [pltpu.SemaphoreType.DMA((len(group),)) for group in (staged, late) if group]
    out_specs = tuple(pl.BlockSpec(memory_space=spaces[place]) for place in out_places)
    pinned = tuple(
        pltpu.HBM(x.shape, x.dtype) if place == "h" else x for x, place in zip(outs, out_places)
    )
    return pl.pallas_call(
        body,
        out_shape=pinned if several else pinned[0],
        in_specs=[pl.BlockSpec(memory_space=spaces[place]) for place in places],
        out_specs=out_specs if several else out_specs[0],
        scratch_shapes=list(scratch) + extra,
        compiler_params=pltpu.CompilerParams(vmem_limit_bytes=room << 20),
        cost_estimate=cost,
    )(*args)


def per_device(
    user_rows, user_row, segment, cand_feat, grad_score, u_weight, v_weight, bias, w_out
):
    user, feat, seg = user_rows[0], cand_feat[0], segment[0]
    peers, replicas = lax.axis_size("dp"), lax.axis_size("replica")
    req, width = user.shape
    rows = feat.shape[0]
    rank = u_weight.shape[1]
    part = width // peers
    piece = width // PIECES
    shape = jax.ShapeDtypeStruct
    bias, w_out = bias[None], w_out[None]
    pairs = [(i, i ^ 1) for i in range(replicas)]
    at = jnp.stack([lax.axis_index("dp"), lax.axis_index("replica") % 2]).astype(jnp.int32)

    message = (peers, PIECES, piece + LANES)
    slots = call(
        request_kernel,
        shape(message, BF16),
        user_row, seg, grad_score, feat,
        places="hhhh",
        scratch=[pltpu.VMEM(message, F32)],
    )
    swap = call(
        swap_kernel,
        shape((16 + req, width), BF16),
        slots, grad_score, user,
        places="ahh",
    )
    arrived = lax.all_to_all(slots, "dp", split_axis=0, concat_axis=0, tiled=True)
    swapped_feat = lax.ppermute(feat, "replica", pairs)
    swapped = lax.ppermute(swap, "replica", pairs)
    base, half, vw, users, user_half, tail = call(
        main_kernel,
        (
            shape((peers, 8, 4 * rank + LANES), BF16),
            shape((width, rank), BF16),
            shape((rank, width), BF16),
            shape((2 * req, width), BF16),
            shape((2 * req, rank), F32),
            shape((part, rank + LANES), F32),
        ),
        at, feat, grad_score, user, swapped_feat, swapped, u_weight, v_weight, bias, w_out,
        scratch=[pltpu.VMEM((2 * rows, width), BF16)],
        places="shhhnnhhhh",
        out_places="nhhnnn",
        cost=pl.CostEstimate(flops=1, bytes_accessed=1, transcendentals=0),
    )
    own = call(
        pick_kernel,
        shape((req, width + LANES), BF16),
        arrived, tail,
        places="-a",
        scratch=[pltpu.VMEM(message, F32)],
    )
    other = lax.ppermute(own, "replica", pairs)
    parts = call(
        merge_kernel,
        shape((peers, 8, 4 * rank + LANES), BF16),
        base, own, other, users, half, user_half,
        places="n--nhn",
    )
    received = lax.all_to_all(parts, "dp", split_axis=0, concat_axis=0, tiled=True)
    user_grad = call(
        user_grad_kernel,
        shape((req, width), F32),
        own, user, u_weight, v_weight, vw, bias, w_out,
        places="-hhhnhh",
    )
    copies = call(sum_kernel, shape((replicas, 8, 4 * rank + LANES), BF16), received)
    gathered = lax.all_to_all(copies, "replica", split_axis=0, concat_axis=0, tiled=True)
    factor = 1.0 / math.sqrt(rows * peers * replicas)
    grad_u, grad_vt, grad_bias, grad_out = call(
        functools.partial(last_kernel, factor),
        (
            shape((part, rank), F32),
            shape((part, rank), F32),
            shape((1, part), F32),
            shape((1, part), F32),
        ),
        gathered, tail,
        places="-n",
    )
    return (user_grad[None], grad_u, grad_vt, grad_bias[0], grad_out[0])


def solution(mesh):
    placed = (
        P("replica", "dp", None),
        P("replica", "dp"),
        P("replica", "dp", None),
        P("replica", "dp", None),
        P("replica", "dp"),
        P(),
        P(),
        P(),
        P(),
    )
    return jax.shard_map(
        per_device,
        mesh=mesh,
        in_specs=placed,
        out_specs=(P("replica", "dp", None), P("dp", None), P("dp", None), P("dp"), P("dp")),
        check_vma=False,
    )
```

```python
import functools
import math

import jax
import jax.numpy as jnp
from jax import lax
from jax.experimental import pallas as pl
from jax.experimental.pallas import tpu as pltpu
from jax.sharding import PartitionSpec as P

F32 = jnp.float32
BF16 = jnp.bfloat16
LANES = 128
PIECES = 2
NT = (((1,), (1,)), ((), ()))
TN = (((0,), (0,)), ((), ()))


def dot(a, b, dims=(((1,), (0,)), ((), ()))):
    return lax.dot_general(a, b, dims, preferred_element_type=F32)


def iota(shape, dim):
    return lax.broadcasted_iota(jnp.int32, shape, dim)


def split_in_two(x):
    high = x.astype(BF16)
    return high, (x - high.astype(F32)).astype(BF16)


def as_columns(row):
    return jnp.transpose(jnp.broadcast_to(row, (LANES, row.shape[1])))


def request_kernel(
    wait, wanted_ref, seg_ref, score_ref, user_ref, feat_ref, slots_ref, pack_ref, wide
):
    peers, req = slots_ref.shape[0], wanted_ref.shape[1]
    rows, width = feat_ref.shape
    piece = width // PIECES
    wait(0, 1, 2)
    wanted = wanted_ref[...]
    owner = lax.div(wanted, jnp.int32(req))
    local = wanted - owner * req
    scores = score_ref[...]
    to_owner = (iota((peers, req), 0) == owner).astype(BF16)
    place = (iota((LANES, req), 0) == local).astype(BF16)
    mine = iota((req, rows), 0) == seg_ref[...]
    total_high, total_low = split_in_two(
        jnp.sum(jnp.where(mine, scores, 0.0), axis=1, keepdims=True)
    )
    lane = iota((req, LANES), 1)
    totals = jnp.where(
        lane == req,
        total_high.astype(F32),
        jnp.where(lane == req + 1, total_low.astype(F32), 0.0),
    ).astype(BF16)
    extra = dot(to_owner, place, NT) + dot(to_owner, totals)
    weights = jnp.where(mine, scores, 0.0).astype(BF16)
    weights = dot(to_owner, weights).astype(BF16)
    wide[:, 0, piece:] = extra
    for p in range(1, PIECES):
        wide[:, p, piece:] = jnp.zeros((peers, LANES), F32)
    score_high, score_low = split_in_two(scores)
    line = iota((16, rows), 0)
    pack_ref[:16, :] = jnp.zeros((16, width), BF16)
    pack_ref[:16, :rows] = jnp.where(
        line == 0,
        score_high.astype(F32),
        jnp.where(line == 1, score_low.astype(F32), 0.0),
    ).astype(BF16)
    wait(3)
    pack_ref[16:, :] = user_ref[...]
    wait(4)
    for p in range(PIECES):
        wide[:, p, :piece] = dot(weights, feat_ref[:, p * piece : (p + 1) * piece])
    slots_ref[...] = wide[...].astype(BF16)


def lay_out(grad, out_ref, base, base_sums):
    peers, rank = out_ref.shape[0], grad.shape[1] - LANES
    blocks = grad.reshape(peers, 4, 8, rank + LANES)
    lane = iota((peers, 8, LANES), 2)
    sums = jnp.zeros((peers, 8, LANES), F32)
    for q in range(4):
        out_ref[:, :, q * rank : (q + 1) * rank] = (blocks[:, q, :, :rank] + base(q)).astype(BF16)
        sums = jnp.where(lane == q, blocks[:, q, :, rank:], sums)
    out_ref[:, :, 4 * rank :] = (sums + base_sums).astype(BF16)


def row_of(ref):
    rows = ref[...].astype(F32)
    return jnp.concatenate([rows[k : k + 1, :] for k in range(rows.shape[0])], axis=1)


def my_core():
    return lax.rem(lax.axis_index("replica"), 2)


def main_kernel(
    wait, feat_any, other_any, score_ref, user_ref, pack_ref, u_ref, v_ref, w_ref,
    base_ref, user_half_ref, next_ref, both, low_ref, sems,
):
    rows, width = feat_any.shape
    rank = v_ref.shape[0]
    req = user_ref.shape[0]
    copies = [
        pltpu.make_async_copy(feat_any, both.at[:rows], sems.at[0]),
        pltpu.make_async_copy(other_any, both.at[rows:], sems.at[1]),
    ]
    for copy in copies:
        copy.start()
    wait(2, 3, 4)
    next_ref[...] = pack_ref[16:, :]
    marks = pack_ref[:16, :rows].astype(F32)
    scores = jnp.concatenate(
        [as_columns(score_ref[...]), as_columns(marks[0:1, :] + marks[1:2, :])], axis=0
    )
    wait(5, 6, 7)
    for copy in copies:
        copy.wait()
    core = my_core()

    @pl.when(core == 0)
    def _():
        u = u_ref[...]
        low_ref[...] = dot(both[...], u)
        user_half_ref[:req, :] = dot(user_ref[...], u)
        user_half_ref[req:, :] = dot(pack_ref[16:, :], u)

    @pl.when(core == 1)
    def _():
        vw = (v_ref[...].astype(F32) * row_of(w_ref)).astype(BF16)
        low_ref[...] = dot(both[...], vw, NT)
        user_half_ref[:req, :] = dot(user_ref[...], vw, NT)
        user_half_ref[req:, :] = dot(pack_ref[16:, :], vw, NT)

    scaled = [low_ref[:, k : k + LANES] * scores for k in range(0, rank, LANES)]
    lane = iota((2 * rows, LANES), 1)
    scaled.append(jnp.where(lane < 4, scores, 0.0))
    scaled = jnp.concatenate(scaled, axis=1).astype(BF16)
    lay_out(dot(both[...], scaled, TN), base_ref, lambda q: 0.0, 0.0)


def pick_kernel(wait, slots_ref, after_any, out_ref, wide):
    req = out_ref.shape[0]
    piece = slots_ref.shape[2] - LANES
    wide[...] = slots_ref[...].astype(F32)
    extra = wide[:, 0, piece:].astype(BF16)
    lane = iota(extra.shape, 1)
    order = jnp.where(lane < req, extra.astype(F32), 0.0).astype(BF16)[:, :req]
    for p in range(PIECES):
        got = wide[:, p, :piece].astype(BF16)
        out_ref[:, p * piece : (p + 1) * piece] = dot(order, got, TN).astype(BF16)
    out_ref[:, PIECES * piece :] = dot(order, extra, TN).astype(BF16)


def total_of(pack, width, req):
    at = width + req
    return pack[:, at : at + 1].astype(F32) + pack[:, at + 1 : at + 2].astype(F32)


def merge_kernel(
    wait, base_ref, own_ref, other_ref, user_ref, next_ref, w_ref, user_half_ref, u_any, v_any,
    out_ref, u_ref, v_ref, both_ref, sem,
):
    req, width = user_ref.shape
    rank = user_half_ref.shape[1]
    core = my_core()
    get_u = pltpu.make_async_copy(u_any, u_ref, sem)
    get_v = pltpu.make_async_copy(v_any, v_ref, sem)

    @pl.when(core == 0)
    def _():
        get_u.start()

    @pl.when(core == 1)
    def _():
        get_v.start()

    own, other = own_ref[...], other_ref[...]
    sums = jnp.concatenate([own[:, :width], other[:, :width]], axis=0)
    total = jnp.concatenate([total_of(own, width, req), total_of(other, width, req)], axis=0)
    wait(3, 4, 5, 6)

    @pl.when(core == 0)
    def _():
        get_u.wait()
        both_ref[...] = dot(sums, u_ref[...])

    @pl.when(core == 1)
    def _():
        get_v.wait()
        weighted = (sums.astype(F32) * row_of(w_ref)).astype(BF16)
        both_ref[...] = dot(weighted, v_ref[...], NT)

    user_half = user_half_ref[...]
    both = both_ref[...] + total * user_half
    lane = iota((2 * req, LANES), 1)
    lines = jnp.concatenate([sums, user_ref[...], next_ref[...]], axis=0)
    factors = jnp.concatenate(
        [
            jnp.concatenate([user_half, jnp.zeros((2 * req, LANES), F32)], axis=1),
            jnp.concatenate([both, jnp.where(lane < 4, total, 0.0)], axis=1),
        ],
        axis=0,
    ).astype(BF16)
    wait(0)
    lay_out(
        dot(lines, factors, TN),
        out_ref,
        lambda q: base_ref[:, :, q * rank : (q + 1) * rank].astype(F32),
        base_ref[:, :, 4 * rank :].astype(F32),
    )


def user_grad_kernel(wait, pack_ref, user_ref, u_ref, v_ref, bias_ref, w_ref, out_ref, tail_ref):
    wait(*range(1, 6))
    req, width = user_ref.shape
    part, rank = tail_ref.shape[0], v_ref.shape[0]
    pack = pack_ref[...]
    sums = pack[:, :width]
    total = total_of(pack, width, req)
    user = user_ref[...]
    u, v = u_ref[...], v_ref[...]
    w_row = row_of(w_ref)
    low = dot(sums, u) + total * dot(user, u)
    both = (jnp.concatenate([sums, user], axis=0).astype(F32) * w_row).astype(BF16)
    both = dot(both, v, NT)
    grad_low = both[:req, :] + total * both[req:, :]
    out_ref[...] = (
        w_row * (dot(low.astype(BF16), v) + total * (bias_ref[...] + 1.0))
        + dot(grad_low.astype(BF16), u, NT)
    )
    here = iota((part, width), 1) == lax.axis_index("dp") * part + iota((part, width), 0)
    tail_ref[:, :rank] = dot(here.astype(BF16), v, NT)
    lane = iota((part, LANES), 1)
    w_col = jnp.sum(jnp.where(here, w_row, 0.0), axis=1, keepdims=True)
    b_col = jnp.sum(jnp.where(here, bias_ref[...], 0.0), axis=1, keepdims=True)
    tail_ref[:, rank:] = jnp.where(lane == 0, w_col, jnp.where(lane == 1, b_col, 0.0))


def sum_kernel(wait, in_ref, out_ref):
    total = jnp.sum(in_ref[...].astype(F32), axis=0).astype(BF16)
    out_ref[...] = jnp.broadcast_to(total[None], out_ref.shape)


def last_kernel(factor, wait, in_ref, tail_ref, grad_u_ref, grad_vt_ref, bias_ref, out_ref):
    wait(1)
    part, rank = grad_u_ref.shape
    replicas = in_ref.shape[0]
    sums = [
        sum(in_ref[k].astype(F32) for k in range(core, replicas, 2)) * factor for core in (0, 1)
    ]
    low, grad_low = (
        jnp.concatenate([s[:, q * rank : (q + 1) * rank] for q in range(4)], axis=0) for s in sums
    )
    column = jnp.concatenate(
        [sums[0][:, 4 * rank + q : 4 * rank + q + 1] for q in range(4)], axis=0
    )
    tail = tail_ref[...]
    w_col, b_col = tail[:, rank : rank + 1], tail[:, rank + 1 : rank + 2]
    grad_u_ref[...] = grad_low
    grad_vt_ref[...] = w_col * low
    out_col = jnp.sum(tail[:, :rank] * low, axis=1, keepdims=True) + (b_col + 1.0) * column
    bias_ref[...] = jnp.transpose(jnp.broadcast_to(w_col * column, (part, LANES)))[0:1, :]
    out_ref[...] = jnp.transpose(jnp.broadcast_to(out_col, (part, LANES)))[0:1, :]


def call(kernel, out, *args, places="", out_places="", scratch=(), room=24, cost=None):
    spaces = {"s": pltpu.SMEM, "a": pl.ANY, "h": pltpu.HBM, "n": pl.ANY, "p": pltpu.HBM, "-": pltpu.VMEM}
    several = isinstance(out, tuple)
    outs = out if several else (out,)
    places = places + "-" * (len(args) - len(places))
    out_places = out_places + "-" * (len(outs) - len(out_places))
    staged = [k for k, place in enumerate(places) if place in "hn"]
    late = [k for k, place in enumerate(out_places) if place in "hn"]
    args = [
        pltpu.with_memory_space_constraint(arg, pltpu.HBM) if place in "hp" else arg
        for arg, place in zip(args, places)
    ]
    n_in, n_out, n_scratch = len(args), len(outs), len(scratch)

    def body(*refs):
        refs = list(refs)
        ins, results = refs[:n_in], refs[n_in : n_in + n_out]
        rest = refs[n_in + n_out :]
        own, rest = rest[:n_scratch], rest[n_scratch:]
        buffers, rest = rest[: len(staged)], rest[len(staged) :]
        out_buffers, rest = rest[: len(late)], rest[len(late) :]
        copies = {}
        for at, k in enumerate(staged):
            copies[k] = pltpu.make_async_copy(ins[k], buffers[at], rest[0].at[at])
            copies[k].start()
            ins[k] = buffers[at]
        targets = {}
        for at, k in enumerate(late):
            targets[k] = results[k]
            results[k] = out_buffers[at]

        def wait(*which):
            for k in which:
                copies.pop(k).wait()

        kernel(wait, *ins, *results, *own)
        assert not copies
        ends = [
            pltpu.make_async_copy(results[k], targets[k], rest[-1].at[at])
            for at, k in enumerate(late)
        ]
        for copy in ends:
            copy.start()
        for copy in ends:
            copy.wait()

    def like(x):
        return pltpu.VMEM(x.shape, x.dtype)

    extra = [like(args[k]) for k in staged] + [like(outs[k]) for k in late]
    extra += [pltpu.SemaphoreType.DMA((len(group),)) for group in (staged, late) if group]
    out_specs = tuple(pl.BlockSpec(memory_space=spaces[place]) for place in out_places)
    pinned = tuple(
        pltpu.HBM(x.shape, x.dtype) if place == "h" else x for x, place in zip(outs, out_places)
    )
    return pl.pallas_call(
        body,
        out_shape=pinned if several else pinned[0],
        in_specs=[pl.BlockSpec(memory_space=spaces[place]) for place in places],
        out_specs=out_specs if several else out_specs[0],
        scratch_shapes=list(scratch) + extra,
        compiler_params=pltpu.CompilerParams(vmem_limit_bytes=room << 20),
        cost_estimate=cost,
    )(*args)


def per_device(
    user_rows, user_row, segment, cand_feat, grad_score, u_weight, v_weight, bias, w_out
):
    user, feat, seg = user_rows[0], cand_feat[0], segment[0]
    peers, replicas = lax.axis_size("dp"), lax.axis_size("replica")
    req, width = user.shape
    rows = feat.shape[0]
    rank = u_weight.shape[1]
    part = width // peers
    piece = width // PIECES
    shape = jax.ShapeDtypeStruct
    bias, w_out = bias[None], w_out.reshape(width // LANES, LANES)
    pairs = [(i, i ^ 1) for i in range(replicas)]
    message = (peers, PIECES, piece + LANES)
    slots, pack = call(
        request_kernel,
        (shape(message, BF16), shape((16 + req, width), BF16)),
        user_row, seg, grad_score, user, feat,
        places="hhhhh",
        scratch=[pltpu.VMEM(message, F32)],
    )
    arrived = lax.all_to_all(slots, "dp", split_axis=0, concat_axis=0, tiled=True)
    swapped_feat = lax.ppermute(feat, "replica", pairs)
    swapped = lax.ppermute(pack, "replica", pairs)
    base, user_half, other_user = call(
        main_kernel,
        (
            shape((peers, 8, 4 * rank + LANES), BF16),
            shape((2 * req, rank), F32),
            shape((req, width), BF16),
        ),
        feat, swapped_feat, grad_score, user, swapped, u_weight, v_weight, w_out,
        places="pahhnhhh",
        out_places="hhh",
        scratch=[
            pltpu.VMEM((2 * rows, width), BF16),
            pltpu.VMEM((2 * rows, rank), F32),
            pltpu.SemaphoreType.DMA((2,)),
        ],
        cost=pl.CostEstimate(flops=1, bytes_accessed=1, transcendentals=0),
    )
    own = call(
        pick_kernel,
        shape((req, width + LANES), BF16),
        arrived, user_half,
        places="-p",
        scratch=[pltpu.VMEM(message, F32)],
    )
    other = lax.ppermute(own, "replica", pairs)
    parts = call(
        merge_kernel,
        shape((peers, 8, 4 * rank + LANES), BF16),
        base, own, other, user, other_user, w_out, user_half, u_weight, v_weight,
        places="h--hhhhpp",
        scratch=[
            pltpu.VMEM((width, rank), BF16),
            pltpu.VMEM((rank, width), BF16),
            pltpu.VMEM((2 * req, rank), F32),
            pltpu.SemaphoreType.DMA,
        ],
    )
    received = lax.all_to_all(parts, "dp", split_axis=0, concat_axis=0, tiled=True)
    user_grad, tail = call(
        user_grad_kernel,
        (shape((req, width), F32), shape((part, rank + LANES), F32)),
        own, user, u_weight, v_weight, bias, w_out,
        places="-hhhhh",
    )
    copies = call(sum_kernel, shape((replicas, 8, 4 * rank + LANES), BF16), received)
    gathered = lax.all_to_all(copies, "replica", split_axis=0, concat_axis=0, tiled=True)
    factor = 1.0 / math.sqrt(rows * peers * replicas)
    grad_u, grad_vt, grad_bias, grad_out = call(
        functools.partial(last_kernel, factor),
        (
            shape((part, rank), F32),
            shape((part, rank), F32),
            shape((1, part), F32),
            shape((1, part), F32),
        ),
        gathered, tail,
        places="-n",
    )
    return (user_grad[None], grad_u, grad_vt, grad_bias[0], grad_out[0])


def solution(mesh):
    placed = (
        P("replica", "dp", None),
        P("replica", "dp"),
        P("replica", "dp", None),
        P("replica", "dp", None),
        P("replica", "dp"),
        P(),
        P(),
        P(),
        P(),
    )
    return jax.shard_map(
        per_device,
        mesh=mesh,
        in_specs=placed,
        out_specs=(P("replica", "dp", None), P("dp", None), P("dp", None), P("dp"), P("dp")),
        check_vma=False,
    )
```

```python
import functools
import math

import jax
import jax.numpy as jnp
from jax import lax
from jax.experimental import pallas as pl
from jax.experimental.pallas import tpu as pltpu
from jax.sharding import PartitionSpec as P

F32 = jnp.float32
BF16 = jnp.bfloat16
LANES = 128
PIECES = 2
NT = (((1,), (1,)), ((), ()))
TN = (((0,), (0,)), ((), ()))


def dot(a, b, dims=(((1,), (0,)), ((), ()))):
    return lax.dot_general(a, b, dims, preferred_element_type=F32)


def iota(shape, dim):
    return lax.broadcasted_iota(jnp.int32, shape, dim)


def split_in_two(x):
    high = x.astype(BF16)
    return high, (x - high.astype(F32)).astype(BF16)


def as_columns(row):
    return jnp.transpose(jnp.broadcast_to(row, (LANES, row.shape[1])))


def request_kernel(
    wait, wanted_ref, seg_ref, score_ref, user_ref, feat_any, slots_ref, pack_ref, wide, feat_ref, sems
):
    peers, req = slots_ref.shape[0], wanted_ref.shape[1]
    rows, width = feat_ref.shape
    piece = width // PIECES
    parts = [pl.ds(p * piece, piece) for p in range(PIECES)]
    copies = [
        pltpu.make_async_copy(feat_any.at[:, part], feat_ref.at[:, part], sems.at[p])
        for p, part in enumerate(parts)
    ]
    for copy in copies:
        copy.start()
    wait(0, 1, 2)
    wanted = wanted_ref[...]
    owner = lax.div(wanted, jnp.int32(req))
    local = wanted - owner * req
    scores = score_ref[...]
    to_owner = (iota((peers, req), 0) == owner).astype(BF16)
    place = (iota((LANES, req), 0) == local).astype(BF16)
    mine = iota((req, rows), 0) == seg_ref[...]
    total_high, total_low = split_in_two(
        jnp.sum(jnp.where(mine, scores, 0.0), axis=1, keepdims=True)
    )
    lane = iota((req, LANES), 1)
    totals = jnp.where(
        lane == req,
        total_high.astype(F32),
        jnp.where(lane == req + 1, total_low.astype(F32), 0.0),
    ).astype(BF16)
    extra = dot(to_owner, place, NT) + dot(to_owner, totals)
    weights = jnp.where(mine, scores, 0.0).astype(BF16)
    weights = dot(to_owner, weights).astype(BF16)
    wide[:, 0, piece:] = extra
    for p in range(1, PIECES):
        wide[:, p, piece:] = jnp.zeros((peers, LANES), F32)
    score_high, score_low = split_in_two(scores)
    line = iota((16, rows), 0)
    pack_ref[:16, :] = jnp.zeros((16, width), BF16)
    pack_ref[:16, :rows] = jnp.where(
        line == 0,
        score_high.astype(F32),
        jnp.where(line == 1, score_low.astype(F32), 0.0),
    ).astype(BF16)
    wait(3)
    pack_ref[16:, :] = user_ref[...]
    for p in range(PIECES):
        copies[p].wait()
        wide[:, p, :piece] = dot(weights, feat_ref[:, p * piece : (p + 1) * piece])
    slots_ref[...] = wide[...].astype(BF16)


def lay_out(grad, sums, out_ref, base):
    peers, rank = out_ref.shape[0], grad.shape[1]
    part = grad.shape[0] // peers
    blocks = grad.reshape(peers, 4, 8, rank)
    for q in range(4):
        out_ref[:, :, q * rank : (q + 1) * rank] = (
            blocks[:, q] + base(slice(q * rank, (q + 1) * rank))
        ).astype(BF16)
    each = LANES // part
    turned = [sums] + [
        jnp.concatenate([sums[:, k * part :], sums[:, : k * part]], axis=1) for k in range(1, each)
    ]
    lines = [
        turned[j % each][:, j // each * LANES : (j // each + 1) * LANES] for j in range(peers)
    ]
    lines = jnp.concatenate([jnp.broadcast_to(line, (8, LANES)) for line in lines], axis=0)
    out_ref[:, :, 4 * rank :] = (
        lines.reshape(peers, 8, LANES) + base(slice(4 * rank, 4 * rank + LANES))
    ).astype(BF16)


def row_of(ref):
    rows = ref[...].astype(F32)
    return jnp.concatenate([rows[k : k + 1, :] for k in range(rows.shape[0])], axis=1)


def my_core():
    return lax.rem(lax.axis_index("replica"), 2)


def get_factor(u_any, v_any, u_ref, v_ref, sem):
    copies = [
        pltpu.make_async_copy(u_any, u_ref, sem),
        pltpu.make_async_copy(v_any, v_ref, sem),
    ]
    core = my_core()
    for k in (0, 1):
        pl.when(core == k)(copies[k].start)
    return copies


def main_kernel(
    wait, feat_any, other_any, score_ref, user_ref, pack_ref, w_ref, u_any, v_any,
    base_ref, user_half_ref, next_ref, both, low_ref, u_ref, v_ref, sems,
):
    rows, width = feat_any.shape
    rank = v_ref.shape[0]
    req = user_ref.shape[0]
    copies = [
        pltpu.make_async_copy(feat_any, both.at[:rows], sems.at[0]),
        pltpu.make_async_copy(other_any, both.at[rows:], sems.at[1]),
    ]
    factors = get_factor(u_any, v_any, u_ref, v_ref, sems.at[2])
    for copy in copies:
        copy.start()
    wait(2, 3, 4, 5)
    next_ref[...] = pack_ref[16:, :]
    marks = pack_ref[:16, :rows].astype(F32)
    scores = jnp.concatenate(
        [as_columns(score_ref[...]), as_columns(marks[0:1, :] + marks[1:2, :])], axis=0
    )
    users = jnp.concatenate([user_ref[...], pack_ref[16:, :]], axis=0)
    core = my_core()

    @pl.when(core == 0)
    def _():
        factors[0].wait()
        user_half_ref[...] = dot(users, u_ref[...])

    @pl.when(core == 1)
    def _():
        factors[1].wait()
        v_ref[...] = (v_ref[...].astype(F32) * row_of(w_ref)).astype(BF16)
        user_half_ref[...] = dot(users, v_ref[...], NT)

    for copy in copies:
        copy.wait()

    @pl.when(core == 0)
    def _():
        low_ref[...] = dot(both[...], u_ref[...])

    @pl.when(core == 1)
    def _():
        low_ref[...] = dot(both[...], v_ref[...], NT)

    scaled = [low_ref[:, k : k + LANES] * scores for k in range(0, rank, LANES)]
    scaled = jnp.concatenate(scaled, axis=1).astype(BF16)
    sums = []
    for k in range(0, width, LANES):
        sums.append(
            jnp.sum(both[:, k : k + LANES].astype(F32) * scores, axis=0, keepdims=True)
        )
    sums = jnp.concatenate(sums, axis=1)
    lay_out(dot(both[...], scaled, TN), sums, base_ref, lambda part: 0.0)


def pick_kernel(wait, slots_ref, after_any, out_ref, wide):
    req = out_ref.shape[0]
    piece = slots_ref.shape[2] - LANES
    wide[...] = slots_ref[...].astype(F32)
    extra = wide[:, 0, piece:].astype(BF16)
    lane = iota(extra.shape, 1)
    order = jnp.where(lane < req, extra.astype(F32), 0.0).astype(BF16)[:, :req]
    for p in range(PIECES):
        got = wide[:, p, :piece].astype(BF16)
        out_ref[:, p * piece : (p + 1) * piece] = dot(order, got, TN).astype(BF16)
    out_ref[:, PIECES * piece :] = dot(order, extra, TN).astype(BF16)


def total_of(pack, width, req):
    at = width + req
    return pack[:, at : at + 1].astype(F32) + pack[:, at + 1 : at + 2].astype(F32)


def merge_kernel(
    wait, own_ref, other_ref, user_ref, next_ref, w_ref, user_half_ref, base_any, u_any, v_any,
    out_ref, base_ref, u_ref, v_ref, both_ref, sems,
):
    req, width = user_ref.shape
    factors = get_factor(u_any, v_any, u_ref, v_ref, sems.at[0])
    get_base = pltpu.make_async_copy(base_any, base_ref, sems.at[1])
    get_base.start()
    own, other = own_ref[...], other_ref[...]
    sums = jnp.concatenate([own[:, :width], other[:, :width]], axis=0)
    total = jnp.concatenate([total_of(own, width, req), total_of(other, width, req)], axis=0)
    wait(2, 3, 4, 5)
    users = jnp.concatenate([user_ref[...], next_ref[...]], axis=0)
    core = my_core()

    @pl.when(core == 0)
    def _():
        factors[0].wait()
        both_ref[...] = dot(sums, u_ref[...])

    @pl.when(core == 1)
    def _():
        weighted = (sums.astype(F32) * row_of(w_ref)).astype(BF16)
        factors[1].wait()
        both_ref[...] = dot(weighted, v_ref[...], NT)

    user_half = user_half_ref[...]
    both = both_ref[...] + total * user_half
    grad = dot(
        jnp.concatenate([sums, users], axis=0),
        jnp.concatenate([user_half, both], axis=0).astype(BF16),
        TN,
    )
    user_sums = jnp.sum(total * users.astype(F32), axis=0, keepdims=True)
    get_base.wait()
    lay_out(grad, user_sums, out_ref, lambda part: base_ref[:, :, part].astype(F32))


def user_grad_kernel(wait, pack_ref, user_ref, u_ref, v_ref, bias_ref, w_ref, out_ref, tail_ref):
    wait(*range(1, 6))
    req, width = user_ref.shape
    part, rank = tail_ref.shape[0], v_ref.shape[0]
    pack = pack_ref[...]
    sums = pack[:, :width]
    total = total_of(pack, width, req)
    user = user_ref[...]
    u, v = u_ref[...], v_ref[...]
    w_row = row_of(w_ref)
    low = dot(sums, u) + total * dot(user, u)
    both = (jnp.concatenate([sums, user], axis=0).astype(F32) * w_row).astype(BF16)
    both = dot(both, v, NT)
    grad_low = both[:req, :] + total * both[req:, :]
    out_ref[...] = (
        w_row * (dot(low.astype(BF16), v) + total * (bias_ref[...] + 1.0))
        + dot(grad_low.astype(BF16), u, NT)
    )
    here = iota((part, width), 1) == lax.axis_index("dp") * part + iota((part, width), 0)
    tail_ref[:, :rank] = dot(here.astype(BF16), v, NT)
    lane = iota((part, LANES), 1)
    w_col = jnp.sum(jnp.where(here, w_row, 0.0), axis=1, keepdims=True)
    b_col = jnp.sum(jnp.where(here, bias_ref[...], 0.0), axis=1, keepdims=True)
    tail_ref[:, rank:] = jnp.where(lane == 0, w_col, jnp.where(lane == 1, b_col, 0.0))


def sum_kernel(wait, in_ref, out_ref):
    total = jnp.sum(in_ref[...].astype(F32), axis=0).astype(BF16)
    out_ref[...] = jnp.broadcast_to(total[None], out_ref.shape)


def last_kernel(factor, wait, in_ref, tail_ref, grad_u_ref, grad_vt_ref, bias_ref, out_ref):
    wait(1)
    part, rank = grad_u_ref.shape
    replicas = in_ref.shape[0]
    sums = [
        sum(in_ref[k].astype(F32) for k in range(core, replicas, 2)) * factor for core in (0, 1)
    ]
    low, grad_low = (
        jnp.concatenate([s[:, q * rank : (q + 1) * rank] for q in range(4)], axis=0) for s in sums
    )
    column = as_columns(sums[0][0:1, 4 * rank :])[:part, 0:1]
    tail = tail_ref[...]
    w_col, b_col = tail[:, rank : rank + 1], tail[:, rank + 1 : rank + 2]
    grad_u_ref[...] = grad_low
    grad_vt_ref[...] = w_col * low
    out_col = jnp.sum(tail[:, :rank] * low, axis=1, keepdims=True) + (b_col + 1.0) * column
    bias_ref[...] = jnp.transpose(jnp.broadcast_to(w_col * column, (part, LANES)))[0:1, :]
    out_ref[...] = jnp.transpose(jnp.broadcast_to(out_col, (part, LANES)))[0:1, :]


def call(kernel, out, *args, places="", out_places="", scratch=(), room=24, cost=None):
    spaces = {"s": pltpu.SMEM, "a": pl.ANY, "h": pltpu.HBM, "n": pl.ANY, "p": pltpu.HBM, "-": pltpu.VMEM}
    several = isinstance(out, tuple)
    outs = out if several else (out,)
    places = places + "-" * (len(args) - len(places))
    out_places = out_places + "-" * (len(outs) - len(out_places))
    staged = [k for k, place in enumerate(places) if place in "hn"]
    late = [k for k, place in enumerate(out_places) if place in "hn"]
    args = [
        pltpu.with_memory_space_constraint(arg, pltpu.HBM) if place in "hp" else arg
        for arg, place in zip(args, places)
    ]
    n_in, n_out, n_scratch = len(args), len(outs), len(scratch)

    def body(*refs):
        refs = list(refs)
        ins, results = refs[:n_in], refs[n_in : n_in + n_out]
        rest = refs[n_in + n_out :]
        own, rest = rest[:n_scratch], rest[n_scratch:]
        buffers, rest = rest[: len(staged)], rest[len(staged) :]
        out_buffers, rest = rest[: len(late)], rest[len(late) :]
        copies = {}
        for at, k in enumerate(staged):
            copies[k] = pltpu.make_async_copy(ins[k], buffers[at], rest[0].at[at])
            copies[k].start()
            ins[k] = buffers[at]
        targets = {}
        for at, k in enumerate(late):
            targets[k] = results[k]
            results[k] = out_buffers[at]

        def wait(*which):
            for k in which:
                copies.pop(k).wait()

        kernel(wait, *ins, *results, *own)
        assert not copies
        ends = [
            pltpu.make_async_copy(results[k], targets[k], rest[-1].at[at])
            for at, k in enumerate(late)
        ]
        for copy in ends:
            copy.start()
        for copy in ends:
            copy.wait()

    def like(x):
        return pltpu.VMEM(x.shape, x.dtype)

    extra = [like(args[k]) for k in staged] + [like(outs[k]) for k in late]
    extra += [pltpu.SemaphoreType.DMA((len(group),)) for group in (staged, late) if group]
    out_specs = tuple(pl.BlockSpec(memory_space=spaces[place]) for place in out_places)
    pinned = tuple(
        pltpu.HBM(x.shape, x.dtype) if place == "h" else x for x, place in zip(outs, out_places)
    )
    return pl.pallas_call(
        body,
        out_shape=pinned if several else pinned[0],
        in_specs=[pl.BlockSpec(memory_space=spaces[place]) for place in places],
        out_specs=out_specs if several else out_specs[0],
        scratch_shapes=list(scratch) + extra,
        compiler_params=pltpu.CompilerParams(vmem_limit_bytes=room << 20),
        cost_estimate=cost,
    )(*args)


def per_device(
    user_rows, user_row, segment, cand_feat, grad_score, u_weight, v_weight, bias, w_out
):
    user, feat, seg = user_rows[0], cand_feat[0], segment[0]
    peers, replicas = lax.axis_size("dp"), lax.axis_size("replica")
    req, width = user.shape
    rows = feat.shape[0]
    rank = u_weight.shape[1]
    part = width // peers
    piece = width // PIECES
    shape = jax.ShapeDtypeStruct
    bias, w_out = bias[None], w_out.reshape(width // LANES, LANES)
    pairs = [(i, i ^ 1) for i in range(replicas)]
    message = (peers, PIECES, piece + LANES)
    slots, pack = call(
        request_kernel,
        (shape(message, BF16), shape((16 + req, width), BF16)),
        user_row, seg, grad_score, user, feat,
        places="hhhhp",
        scratch=[
            pltpu.VMEM(message, F32),
            pltpu.VMEM((rows, width), BF16),
            pltpu.SemaphoreType.DMA((PIECES,)),
        ],
    )
    arrived = lax.all_to_all(slots, "dp", split_axis=0, concat_axis=0, tiled=True)
    swapped_feat = lax.ppermute(feat, "replica", pairs)
    swapped = lax.ppermute(pack, "replica", pairs)
    factor_buffers = [pltpu.VMEM((width, rank), BF16), pltpu.VMEM((rank, width), BF16)]
    parts_shape = (peers, 8, 4 * rank + LANES)
    base, user_half, other_user = call(
        main_kernel,
        (
            shape(parts_shape, BF16),
            shape((2 * req, rank), F32),
            shape((req, width), BF16),
        ),
        feat, swapped_feat, grad_score, user, swapped, w_out, u_weight, v_weight,
        places="pahhnhpp",
        out_places="hhh",
        scratch=[
            pltpu.VMEM((2 * rows, width), BF16),
            pltpu.VMEM((2 * rows, rank), F32),
            *factor_buffers,
            pltpu.SemaphoreType.DMA((3,)),
        ],
        cost=pl.CostEstimate(flops=1, bytes_accessed=1, transcendentals=0),
    )
    own = call(
        pick_kernel,
        shape((req, width + LANES), BF16),
        arrived, user_half,
        places="-p",
        scratch=[pltpu.VMEM(message, F32)],
    )
    other = lax.ppermute(own, "replica", pairs)
    parts = call(
        merge_kernel,
        shape(parts_shape, BF16),
        own, other, user, other_user, w_out, user_half, base, u_weight, v_weight,
        places="--hhhhppp",
        scratch=[
            pltpu.VMEM(parts_shape, BF16),
            *factor_buffers,
            pltpu.VMEM((2 * req, rank), F32),
            pltpu.SemaphoreType.DMA((2,)),
        ],
    )
    received = lax.all_to_all(parts, "dp", split_axis=0, concat_axis=0, tiled=True)
    user_grad, tail = call(
        user_grad_kernel,
        (shape((req, width), F32), shape((part, rank + LANES), F32)),
        own, user, u_weight, v_weight, bias, w_out,
        places="-hhhhh",
    )
    copies = call(sum_kernel, shape((replicas, 8, 4 * rank + LANES), BF16), received)
    gathered = lax.all_to_all(copies, "replica", split_axis=0, concat_axis=0, tiled=True)
    factor = 1.0 / math.sqrt(rows * peers * replicas)
    grad_u, grad_vt, grad_bias, grad_out = call(
        functools.partial(last_kernel, factor),
        (
            shape((part, rank), F32),
            shape((part, rank), F32),
            shape((1, part), F32),
            shape((1, part), F32),
        ),
        gathered, tail,
        places="-n",
    )
    return (user_grad[None], grad_u, grad_vt, grad_bias[0], grad_out[0])


def solution(mesh):
    placed = (
        P("replica", "dp", None),
        P("replica", "dp"),
        P("replica", "dp", None),
        P("replica", "dp", None),
        P("replica", "dp"),
        P(),
        P(),
        P(),
        P(),
    )
    return jax.shard_map(
        per_device,
        mesh=mesh,
        in_specs=placed,
        out_specs=(P("replica", "dp", None), P("dp", None), P("dp", None), P("dp"), P("dp")),
        check_vma=False,
    )
```

```python
import functools
import math

import jax
import jax.numpy as jnp
from jax import lax
from jax.experimental import pallas as pl
from jax.experimental.pallas import tpu as pltpu
from jax.sharding import PartitionSpec as P

F32 = jnp.float32
BF16 = jnp.bfloat16
LANES = 128
PIECES = 2
NT = (((1,), (1,)), ((), ()))
TN = (((0,), (0,)), ((), ()))


def dot(a, b, dims=(((1,), (0,)), ((), ()))):
    return lax.dot_general(a, b, dims, preferred_element_type=F32)


def iota(shape, dim):
    return lax.broadcasted_iota(jnp.int32, shape, dim)


def split_in_two(x):
    high = x.astype(BF16)
    return high, (x - high.astype(F32)).astype(BF16)


def as_columns(row):
    return jnp.transpose(jnp.broadcast_to(row, (LANES, row.shape[1])))


def request_kernel(
    wait, wanted_ref, seg_ref, score_ref, user_ref, feat_any, slots_ref, pack_ref, wide, feat_ref, sems
):
    peers, req = slots_ref.shape[0], wanted_ref.shape[1]
    rows, width = feat_ref.shape
    piece = width // PIECES
    parts = [pl.ds(p * piece, piece) for p in range(PIECES)]
    copies = [
        pltpu.make_async_copy(feat_any.at[:, part], feat_ref.at[:, part], sems.at[p])
        for p, part in enumerate(parts)
    ]
    for copy in copies:
        copy.start()
    wait(0, 1, 2)
    wanted = wanted_ref[...]
    owner = lax.div(wanted, jnp.int32(req))
    local = wanted - owner * req
    scores = score_ref[...]
    to_owner = (iota((peers, req), 0) == owner).astype(BF16)
    place = (iota((LANES, req), 0) == local).astype(BF16)
    mine = iota((req, rows), 0) == seg_ref[...]
    total_high, total_low = split_in_two(
        jnp.sum(jnp.where(mine, scores, 0.0), axis=1, keepdims=True)
    )
    lane = iota((req, LANES), 1)
    totals = jnp.where(
        lane == req,
        total_high.astype(F32),
        jnp.where(lane == req + 1, total_low.astype(F32), 0.0),
    ).astype(BF16)
    extra = dot(to_owner, place, NT) + dot(to_owner, totals)
    weights = jnp.where(mine, scores, 0.0).astype(BF16)
    weights = dot(to_owner, weights).astype(BF16)
    wide[:, 0, piece:] = extra
    for p in range(1, PIECES):
        wide[:, p, piece:] = jnp.zeros((peers, LANES), F32)
    score_high, score_low = split_in_two(scores)
    line = iota((16, rows), 0)
    pack_ref[:16, :] = jnp.zeros((16, width), BF16)
    pack_ref[:16, :rows] = jnp.where(
        line == 0,
        score_high.astype(F32),
        jnp.where(line == 1, score_low.astype(F32), 0.0),
    ).astype(BF16)
    wait(3)
    pack_ref[16:, :] = user_ref[...]
    for p in range(PIECES):
        copies[p].wait()
        wide[:, p, :piece] = dot(weights, feat_ref[:, p * piece : (p + 1) * piece])
    slots_ref[...] = wide[...].astype(BF16)


def lay_out(grad, sums, out_ref, base):
    peers, rank = out_ref.shape[0], grad.shape[1]
    part = grad.shape[0] // peers
    blocks = grad.reshape(peers, 4, 8, rank)
    for q in range(4):
        out_ref[:, :, q * rank : (q + 1) * rank] = (
            blocks[:, q] + base(slice(q * rank, (q + 1) * rank))
        ).astype(BF16)
    each = LANES // part
    turned = [sums] + [
        jnp.concatenate([sums[:, k * part :], sums[:, : k * part]], axis=1) for k in range(1, each)
    ]
    lines = [
        turned[j % each][:, j // each * LANES : (j // each + 1) * LANES] for j in range(peers)
    ]
    lines = jnp.concatenate([jnp.broadcast_to(line, (8, LANES)) for line in lines], axis=0)
    out_ref[:, :, 4 * rank :] = (
        lines.reshape(peers, 8, LANES) + base(slice(4 * rank, 4 * rank + LANES))
    ).astype(BF16)


def row_of(ref):
    rows = ref[...].astype(F32)
    return jnp.concatenate([rows[k : k + 1, :] for k in range(rows.shape[0])], axis=1)


def my_core():
    return lax.rem(lax.axis_index("replica"), 2)


def main_kernel(
    wait, feat_any, other_any, score_ref, user_ref, pack_ref, w_ref, u_any, v_any,
    base_ref, half_ref, user_half_ref, users_ref, both, v_ref, sems,
):
    rows, width = feat_any.shape
    rank = v_ref.shape[0]
    req = user_ref.shape[0]
    core = my_core()
    get_u = pltpu.make_async_copy(u_any, half_ref, sems.at[0])
    get_v = pltpu.make_async_copy(v_any, v_ref, sems.at[0])
    copies = [
        pltpu.make_async_copy(feat_any, both.at[:rows], sems.at[1]),
        pltpu.make_async_copy(other_any, both.at[rows:], sems.at[2]),
    ]
    pl.when(core == 0)(get_u.start)
    pl.when(core == 1)(get_v.start)
    for copy in copies:
        copy.start()
    wait(2, 3, 4, 5)
    users_ref[:req, :] = user_ref[...]
    users_ref[req:, :] = pack_ref[16:, :]
    marks = pack_ref[:16, :rows].astype(F32)
    scores = jnp.concatenate(
        [as_columns(score_ref[...]), as_columns(marks[0:1, :] + marks[1:2, :])], axis=0
    )
    pl.when(core == 0)(get_u.wait)

    @pl.when(core == 1)
    def _():
        get_v.wait()
        half_ref[...] = jnp.transpose((v_ref[...].astype(F32) * row_of(w_ref)).astype(BF16))

    half = half_ref[...]
    user_half_ref[...] = dot(users_ref[...], half)
    scaled, sums = [], []
    for at, copy in zip((0, rows), copies):
        copy.wait()
        here, weight = both[at : at + rows, :], scores[at : at + rows, :]
        low = dot(here, half)
        scaled.append(
            jnp.concatenate(
                [low[:, k : k + LANES] * weight for k in range(0, rank, LANES)], axis=1
            ).astype(BF16)
        )
        sums.append(
            jnp.concatenate(
                [
                    jnp.sum(here[:, k : k + LANES].astype(F32) * weight, axis=0, keepdims=True)
                    for k in range(0, width, LANES)
                ],
                axis=1,
            )
        )
    grad = dot(both[...], jnp.concatenate(scaled, axis=0), TN)
    lay_out(grad, sums[0] + sums[1], base_ref, lambda part: 0.0)


def pick_kernel(wait, slots_ref, after_any, out_ref, wide):
    req = out_ref.shape[0]
    piece = slots_ref.shape[2] - LANES
    wide[...] = slots_ref[...].astype(F32)
    extra = wide[:, 0, piece:].astype(BF16)
    lane = iota(extra.shape, 1)
    order = jnp.where(lane < req, extra.astype(F32), 0.0).astype(BF16)[:, :req]
    for p in range(PIECES):
        got = wide[:, p, :piece].astype(BF16)
        out_ref[:, p * piece : (p + 1) * piece] = dot(order, got, TN).astype(BF16)
    out_ref[:, PIECES * piece :] = dot(order, extra, TN).astype(BF16)


def total_of(pack, width, req):
    at = width + req
    return pack[:, at : at + 1].astype(F32) + pack[:, at + 1 : at + 2].astype(F32)


def merge_kernel(wait, own_ref, other_ref, users_ref, half_ref, user_half_ref, base_ref, out_ref):
    req, width = users_ref.shape[0] // 2, users_ref.shape[1]
    own, other = own_ref[...], other_ref[...]
    sums = jnp.concatenate([own[:, :width], other[:, :width]], axis=0)
    total = jnp.concatenate([total_of(own, width, req), total_of(other, width, req)], axis=0)
    users, user_half = users_ref[...], user_half_ref[...]
    both = dot(sums, half_ref[...]) + total * user_half
    grad = dot(
        jnp.concatenate([sums, users], axis=0),
        jnp.concatenate([user_half, both], axis=0).astype(BF16),
        TN,
    )
    wait(5)
    user_sums = jnp.sum(total * users.astype(F32), axis=0, keepdims=True)
    lay_out(grad, user_sums, out_ref, lambda part: base_ref[:, :, part].astype(F32))


def user_grad_kernel(wait, pack_ref, user_ref, u_ref, v_ref, bias_ref, w_ref, out_ref, tail_ref):
    wait(*range(1, 6))
    req, width = user_ref.shape
    part, rank = tail_ref.shape[0], v_ref.shape[0]
    pack = pack_ref[...]
    sums = pack[:, :width]
    total = total_of(pack, width, req)
    user = user_ref[...]
    u, v = u_ref[...], v_ref[...]
    w_row = row_of(w_ref)
    low = dot(sums, u) + total * dot(user, u)
    both = (jnp.concatenate([sums, user], axis=0).astype(F32) * w_row).astype(BF16)
    both = dot(both, v, NT)
    grad_low = both[:req, :] + total * both[req:, :]
    out_ref[...] = (
        w_row * (dot(low.astype(BF16), v) + total * (bias_ref[...] + 1.0))
        + dot(grad_low.astype(BF16), u, NT)
    )
    here = iota((part, width), 1) == lax.axis_index("dp") * part + iota((part, width), 0)
    tail_ref[:, :rank] = dot(here.astype(BF16), v, NT)
    lane = iota((part, LANES), 1)
    w_col = jnp.sum(jnp.where(here, w_row, 0.0), axis=1, keepdims=True)
    b_col = jnp.sum(jnp.where(here, bias_ref[...], 0.0), axis=1, keepdims=True)
    tail_ref[:, rank:] = jnp.where(lane == 0, w_col, jnp.where(lane == 1, b_col, 0.0))


def sum_kernel(wait, in_ref, out_ref):
    total = jnp.sum(in_ref[...].astype(F32), axis=0).astype(BF16)
    out_ref[...] = jnp.broadcast_to(total[None], out_ref.shape)


def last_kernel(factor, wait, in_ref, tail_ref, grad_u_ref, grad_vt_ref, bias_ref, out_ref):
    wait(1)
    part, rank = grad_u_ref.shape
    replicas = in_ref.shape[0]
    sums = [
        sum(in_ref[k].astype(F32) for k in range(core, replicas, 2)) * factor for core in (0, 1)
    ]
    low, grad_low = (
        jnp.concatenate([s[:, q * rank : (q + 1) * rank] for q in range(4)], axis=0) for s in sums
    )
    column = as_columns(sums[0][0:1, 4 * rank :])[:part, 0:1]
    tail = tail_ref[...]
    w_col, b_col = tail[:, rank : rank + 1], tail[:, rank + 1 : rank + 2]
    grad_u_ref[...] = grad_low
    grad_vt_ref[...] = w_col * low
    out_col = jnp.sum(tail[:, :rank] * low, axis=1, keepdims=True) + (b_col + 1.0) * column
    bias_ref[...] = jnp.transpose(jnp.broadcast_to(w_col * column, (part, LANES)))[0:1, :]
    out_ref[...] = jnp.transpose(jnp.broadcast_to(out_col, (part, LANES)))[0:1, :]


def call(kernel, out, *args, places="", out_places="", scratch=(), room=24, cost=None):
    spaces = {"s": pltpu.SMEM, "a": pl.ANY, "h": pltpu.HBM, "n": pl.ANY, "p": pltpu.HBM, "-": pltpu.VMEM}
    several = isinstance(out, tuple)
    outs = out if several else (out,)
    places = places + "-" * (len(args) - len(places))
    out_places = out_places + "-" * (len(outs) - len(out_places))
    staged = [k for k, place in enumerate(places) if place in "hn"]
    late = [k for k, place in enumerate(out_places) if place in "hn"]
    args = [
        pltpu.with_memory_space_constraint(arg, pltpu.HBM) if place in "hp" else arg
        for arg, place in zip(args, places)
    ]
    n_in, n_out, n_scratch = len(args), len(outs), len(scratch)

    def body(*refs):
        refs = list(refs)
        ins, results = refs[:n_in], refs[n_in : n_in + n_out]
        rest = refs[n_in + n_out :]
        own, rest = rest[:n_scratch], rest[n_scratch:]
        buffers, rest = rest[: len(staged)], rest[len(staged) :]
        out_buffers, rest = rest[: len(late)], rest[len(late) :]
        copies = {}
        for at, k in enumerate(staged):
            copies[k] = pltpu.make_async_copy(ins[k], buffers[at], rest[0].at[at])
            copies[k].start()
            ins[k] = buffers[at]
        targets = {}
        for at, k in enumerate(late):
            targets[k] = results[k]
            results[k] = out_buffers[at]

        def wait(*which):
            for k in which:
                copies.pop(k).wait()

        kernel(wait, *ins, *results, *own)
        assert not copies
        ends = [
            pltpu.make_async_copy(results[k], targets[k], rest[-1].at[at])
            for at, k in enumerate(late)
        ]
        for copy in ends:
            copy.start()
        for copy in ends:
            copy.wait()

    def like(x):
        return pltpu.VMEM(x.shape, x.dtype)

    extra = [like(args[k]) for k in staged] + [like(outs[k]) for k in late]
    extra += [pltpu.SemaphoreType.DMA((len(group),)) for group in (staged, late) if group]
    out_specs = tuple(pl.BlockSpec(memory_space=spaces[place]) for place in out_places)
    pinned = tuple(
        pltpu.HBM(x.shape, x.dtype) if place == "h" else x for x, place in zip(outs, out_places)
    )
    return pl.pallas_call(
        body,
        out_shape=pinned if several else pinned[0],
        in_specs=[pl.BlockSpec(memory_space=spaces[place]) for place in places],
        out_specs=out_specs if several else out_specs[0],
        scratch_shapes=list(scratch) + extra,
        compiler_params=pltpu.CompilerParams(vmem_limit_bytes=room << 20),
        cost_estimate=cost,
    )(*args)


def per_device(
    user_rows, user_row, segment, cand_feat, grad_score, u_weight, v_weight, bias, w_out
):
    user, feat, seg = user_rows[0], cand_feat[0], segment[0]
    peers, replicas = lax.axis_size("dp"), lax.axis_size("replica")
    req, width = user.shape
    rows = feat.shape[0]
    rank = u_weight.shape[1]
    part = width // peers
    piece = width // PIECES
    shape = jax.ShapeDtypeStruct
    bias, w_out = bias[None], w_out.reshape(width // LANES, LANES)
    pairs = [(i, i ^ 1) for i in range(replicas)]
    message = (peers, PIECES, piece + LANES)
    slots, pack = call(
        request_kernel,
        (shape(message, BF16), shape((16 + req, width), BF16)),
        user_row, seg, grad_score, user, feat,
        places="hhhhp",
        scratch=[
            pltpu.VMEM(message, F32),
            pltpu.VMEM((rows, width), BF16),
            pltpu.SemaphoreType.DMA((PIECES,)),
        ],
    )
    arrived = lax.all_to_all(slots, "dp", split_axis=0, concat_axis=0, tiled=True)
    swapped_feat = lax.ppermute(feat, "replica", pairs)
    swapped = lax.ppermute(pack, "replica", pairs)
    parts_shape = (peers, 8, 4 * rank + LANES)
    base, half, user_half, users = call(
        main_kernel,
        (
            shape(parts_shape, BF16),
            shape((width, rank), BF16),
            shape((2 * req, rank), F32),
            shape((2 * req, width), BF16),
        ),
        feat, swapped_feat, grad_score, user, swapped, w_out, u_weight, v_weight,
        places="pahhnhpp",
        out_places="h",
        scratch=[
            pltpu.VMEM((2 * rows, width), BF16),
            pltpu.VMEM((rank, width), BF16),
            pltpu.SemaphoreType.DMA((3,)),
        ],
        cost=pl.CostEstimate(flops=1, bytes_accessed=1, transcendentals=0),
    )
    own = call(
        pick_kernel,
        shape((req, width + LANES), BF16),
        arrived, user_half,
        places="-a",
        scratch=[pltpu.VMEM(message, F32)],
    )
    other = lax.ppermute(own, "replica", pairs)
    parts = call(
        merge_kernel,
        shape(parts_shape, BF16),
        own, other, users, half, user_half, base,
        places="-----h",
    )
    received = lax.all_to_all(parts, "dp", split_axis=0, concat_axis=0, tiled=True)
    user_grad, tail = call(
        user_grad_kernel,
        (shape((req, width), F32), shape((part, rank + LANES), F32)),
        own, user, u_weight, v_weight, bias, w_out,
        places="-hhhhh",
    )
    copies = call(sum_kernel, shape((replicas, 8, 4 * rank + LANES), BF16), received)
    gathered = lax.all_to_all(copies, "replica", split_axis=0, concat_axis=0, tiled=True)
    factor = 1.0 / math.sqrt(rows * peers * replicas)
    grad_u, grad_vt, grad_bias, grad_out = call(
        functools.partial(last_kernel, factor),
        (
            shape((part, rank), F32),
            shape((part, rank), F32),
            shape((1, part), F32),
            shape((1, part), F32),
        ),
        gathered, tail,
        places="-n",
    )
    return (user_grad[None], grad_u, grad_vt, grad_bias[0], grad_out[0])


def solution(mesh):
    placed = (
        P("replica", "dp", None),
        P("replica", "dp"),
        P("replica", "dp", None),
        P("replica", "dp", None),
        P("replica", "dp"),
        P(),
        P(),
        P(),
        P(),
    )
    return jax.shard_map(
        per_device,
        mesh=mesh,
        in_specs=placed,
        out_specs=(P("replica", "dp", None), P("dp", None), P("dp", None), P("dp"), P("dp")),
        check_vma=False,
    )
```

```python
import functools
import math

import jax
import jax.numpy as jnp
from jax import lax
from jax.experimental import pallas as pl
from jax.experimental.pallas import tpu as pltpu
from jax.sharding import PartitionSpec as P

F32 = jnp.float32
BF16 = jnp.bfloat16
LANES = 128
PIECES = 2
TURN = 36 / 64
NT = (((1,), (1,)), ((), ()))
TN = (((0,), (0,)), ((), ()))


def dot(a, b, dims=(((1,), (0,)), ((), ()))):
    return lax.dot_general(a, b, dims, preferred_element_type=F32)


def iota(shape, dim):
    return lax.broadcasted_iota(jnp.int32, shape, dim)


def split_in_two(x):
    high = x.astype(BF16)
    return high, (x - high.astype(F32)).astype(BF16)


def as_columns(row):
    return jnp.transpose(jnp.broadcast_to(row, (LANES, row.shape[1])))


def request_kernel(
    wait, wanted_ref, seg_ref, score_ref, user_ref, feat_any, slots_ref, pack_ref, wide, feat_ref, sems
):
    peers, req = slots_ref.shape[0], wanted_ref.shape[1]
    rows, width = feat_ref.shape
    piece = width // PIECES
    parts = [pl.ds(p * piece, piece) for p in range(PIECES)]
    copies = [
        pltpu.make_async_copy(feat_any.at[:, part], feat_ref.at[:, part], sems.at[p])
        for p, part in enumerate(parts)
    ]
    for copy in copies:
        copy.start()
    wait(0, 1, 2)
    wanted = wanted_ref[...]
    owner = lax.div(wanted, jnp.int32(req))
    local = wanted - owner * req
    scores = score_ref[...]
    turn = round(TURN * peers)
    to_owner = (iota((peers, req), 0) == lax.rem(owner + (peers - turn), peers)).astype(BF16)
    place = (iota((LANES, req), 0) == local).astype(BF16)
    mine = iota((req, rows), 0) == seg_ref[...]
    total_high, total_low = split_in_two(
        jnp.sum(jnp.where(mine, scores, 0.0), axis=1, keepdims=True)
    )
    lane = iota((req, LANES), 1)
    totals = jnp.where(
        lane == req,
        total_high.astype(F32),
        jnp.where(lane == req + 1, total_low.astype(F32), 0.0),
    ).astype(BF16)
    extra = dot(to_owner, place, NT) + dot(to_owner, totals)
    weights = jnp.where(mine, scores, 0.0).astype(BF16)
    weights = dot(to_owner, weights).astype(BF16)
    wide[:, 0, piece:] = extra
    for p in range(1, PIECES):
        wide[:, p, piece:] = jnp.zeros((peers, LANES), F32)
    score_high, score_low = split_in_two(scores)
    line = iota((16, rows), 0)
    pack_ref[:16, :] = jnp.zeros((16, width), BF16)
    pack_ref[:16, :rows] = jnp.where(
        line == 0,
        score_high.astype(F32),
        jnp.where(line == 1, score_low.astype(F32), 0.0),
    ).astype(BF16)
    wait(3)
    pack_ref[16:, :] = user_ref[...]
    for p in range(PIECES):
        copies[p].wait()
        wide[:, p, :piece] = dot(weights, feat_ref[:, p * piece : (p + 1) * piece])
    slots_ref[...] = wide[...].astype(BF16)


def lay_out(grad, sums, out_ref, base):
    peers, rank = out_ref.shape[0], grad.shape[1]
    part = grad.shape[0] // peers
    turn = round(TURN * peers)
    order = [(j + turn) % peers for j in range(peers)]
    blocks = grad.reshape(peers, 4, 8, rank)
    blocks = jnp.concatenate([blocks[turn:], blocks[:turn]], axis=0)
    for q in range(4):
        out_ref[:, :, q * rank : (q + 1) * rank] = (
            blocks[:, q] + base(slice(q * rank, (q + 1) * rank))
        ).astype(BF16)
    each = LANES // part
    turned = [sums] + [
        jnp.concatenate([sums[:, k * part :], sums[:, : k * part]], axis=1) for k in range(1, each)
    ]
    lines = [
        turned[j % each][:, j // each * LANES : (j // each + 1) * LANES] for j in order
    ]
    lines = jnp.concatenate([jnp.broadcast_to(line, (8, LANES)) for line in lines], axis=0)
    out_ref[:, :, 4 * rank :] = (
        lines.reshape(peers, 8, LANES) + base(slice(4 * rank, 4 * rank + LANES))
    ).astype(BF16)


def row_of(ref):
    rows = ref[...].astype(F32)
    return jnp.concatenate([rows[k : k + 1, :] for k in range(rows.shape[0])], axis=1)


def my_core():
    return lax.rem(lax.axis_index("replica"), 2)


def main_kernel(
    wait, feat_any, other_any, score_ref, user_ref, pack_ref, w_ref, u_any, v_any,
    base_ref, half_ref, user_half_ref, users_ref, both, v_ref, sems,
):
    rows, width = feat_any.shape
    rank = v_ref.shape[0]
    req = user_ref.shape[0]
    core = my_core()
    get_u = pltpu.make_async_copy(u_any, half_ref, sems.at[0])
    get_v = pltpu.make_async_copy(v_any, v_ref, sems.at[0])
    copies = [
        pltpu.make_async_copy(feat_any, both.at[:rows], sems.at[1]),
        pltpu.make_async_copy(other_any, both.at[rows:], sems.at[2]),
    ]
    pl.when(core == 0)(get_u.start)
    pl.when(core == 1)(get_v.start)
    for copy in copies:
        copy.start()
    wait(2, 3, 4, 5)
    users_ref[:req, :] = user_ref[...]
    users_ref[req:, :] = pack_ref[16:, :]
    marks = pack_ref[:16, :rows].astype(F32)
    scores = jnp.concatenate(
        [as_columns(score_ref[...]), as_columns(marks[0:1, :] + marks[1:2, :])], axis=0
    )
    pl.when(core == 0)(get_u.wait)

    @pl.when(core == 1)
    def _():
        get_v.wait()
        half_ref[...] = jnp.transpose((v_ref[...].astype(F32) * row_of(w_ref)).astype(BF16))

    half = half_ref[...]
    user_half_ref[...] = dot(users_ref[...], half)
    scaled, sums = [], []
    for at, copy in zip((0, rows), copies):
        copy.wait()
        here, weight = both[at : at + rows, :], scores[at : at + rows, :]
        low = dot(here, half)
        scaled.append(
            jnp.concatenate(
                [low[:, k : k + LANES] * weight for k in range(0, rank, LANES)], axis=1
            ).astype(BF16)
        )
        sums.append(
            jnp.concatenate(
                [
                    jnp.sum(here[:, k : k + LANES].astype(F32) * weight, axis=0, keepdims=True)
                    for k in range(0, width, LANES)
                ],
                axis=1,
            )
        )
    grad = dot(both[...], jnp.concatenate(scaled, axis=0), TN)
    lay_out(grad, sums[0] + sums[1], base_ref, lambda part: 0.0)


def pick_kernel(wait, slots_ref, after_any, out_ref, wide):
    req = out_ref.shape[0]
    piece = slots_ref.shape[2] - LANES
    wide[...] = slots_ref[...].astype(F32)
    extra = wide[:, 0, piece:].astype(BF16)
    lane = iota(extra.shape, 1)
    order = jnp.where(lane < req, extra.astype(F32), 0.0).astype(BF16)[:, :req]
    for p in range(PIECES):
        got = wide[:, p, :piece].astype(BF16)
        out_ref[:, p * piece : (p + 1) * piece] = dot(order, got, TN).astype(BF16)
    out_ref[:, PIECES * piece :] = dot(order, extra, TN).astype(BF16)


def total_of(pack, width, req):
    at = width + req
    return pack[:, at : at + 1].astype(F32) + pack[:, at + 1 : at + 2].astype(F32)


def merge_kernel(wait, own_ref, other_ref, users_ref, half_ref, user_half_ref, base_ref, out_ref):
    req, width = users_ref.shape[0] // 2, users_ref.shape[1]
    own, other = own_ref[...], other_ref[...]
    sums = jnp.concatenate([own[:, :width], other[:, :width]], axis=0)
    total = jnp.concatenate([total_of(own, width, req), total_of(other, width, req)], axis=0)
    users, user_half = users_ref[...], user_half_ref[...]
    both = dot(sums, half_ref[...]) + total * user_half
    grad = dot(
        jnp.concatenate([sums, users], axis=0),
        jnp.concatenate([user_half, both], axis=0).astype(BF16),
        TN,
    )
    wait(5)
    user_sums = jnp.sum(total * users.astype(F32), axis=0, keepdims=True)
    lay_out(grad, user_sums, out_ref, lambda part: base_ref[:, :, part].astype(F32))


def user_grad_kernel(wait, pack_ref, user_ref, u_ref, v_ref, bias_ref, w_ref, out_ref, tail_ref):
    wait(*range(1, 6))
    req, width = user_ref.shape
    part, rank = tail_ref.shape[0], v_ref.shape[0]
    pack = pack_ref[...]
    sums = pack[:, :width]
    total = total_of(pack, width, req)
    user = user_ref[...]
    u, v = u_ref[...], v_ref[...]
    w_row = row_of(w_ref)
    low = dot(sums, u) + total * dot(user, u)
    both = (jnp.concatenate([sums, user], axis=0).astype(F32) * w_row).astype(BF16)
    both = dot(both, v, NT)
    grad_low = both[:req, :] + total * both[req:, :]
    out_ref[...] = (
        w_row * (dot(low.astype(BF16), v) + total * (bias_ref[...] + 1.0))
        + dot(grad_low.astype(BF16), u, NT)
    )
    here = iota((part, width), 1) == lax.axis_index("dp") * part + iota((part, width), 0)
    tail_ref[:, :rank] = dot(here.astype(BF16), v, NT)
    lane = iota((part, LANES), 1)
    w_col = jnp.sum(jnp.where(here, w_row, 0.0), axis=1, keepdims=True)
    b_col = jnp.sum(jnp.where(here, bias_ref[...], 0.0), axis=1, keepdims=True)
    tail_ref[:, rank:] = jnp.where(lane == 0, w_col, jnp.where(lane == 1, b_col, 0.0))


def sum_kernel(wait, in_ref, out_ref):
    total = jnp.sum(in_ref[...].astype(F32), axis=0).astype(BF16)
    out_ref[...] = jnp.broadcast_to(total[None], out_ref.shape)


def last_kernel(factor, wait, in_ref, tail_ref, grad_u_ref, grad_vt_ref, bias_ref, out_ref):
    wait(1)
    part, rank = grad_u_ref.shape
    replicas = in_ref.shape[0]
    sums = [
        sum(in_ref[k].astype(F32) for k in range(core, replicas, 2)) * factor for core in (0, 1)
    ]
    low, grad_low = (
        jnp.concatenate([s[:, q * rank : (q + 1) * rank] for q in range(4)], axis=0) for s in sums
    )
    column = as_columns(sums[0][0:1, 4 * rank :])[:part, 0:1]
    tail = tail_ref[...]
    w_col, b_col = tail[:, rank : rank + 1], tail[:, rank + 1 : rank + 2]
    grad_u_ref[...] = grad_low
    grad_vt_ref[...] = w_col * low
    out_col = jnp.sum(tail[:, :rank] * low, axis=1, keepdims=True) + (b_col + 1.0) * column
    bias_ref[...] = jnp.transpose(jnp.broadcast_to(w_col * column, (part, LANES)))[0:1, :]
    out_ref[...] = jnp.transpose(jnp.broadcast_to(out_col, (part, LANES)))[0:1, :]


def call(kernel, out, *args, places="", out_places="", scratch=(), room=24, cost=None):
    spaces = {"s": pltpu.SMEM, "a": pl.ANY, "h": pltpu.HBM, "n": pl.ANY, "p": pltpu.HBM, "-": pltpu.VMEM}
    several = isinstance(out, tuple)
    outs = out if several else (out,)
    places = places + "-" * (len(args) - len(places))
    out_places = out_places + "-" * (len(outs) - len(out_places))
    staged = [k for k, place in enumerate(places) if place in "hn"]
    late = [k for k, place in enumerate(out_places) if place in "hn"]
    args = [
        pltpu.with_memory_space_constraint(arg, pltpu.HBM) if place in "hp" else arg
        for arg, place in zip(args, places)
    ]
    n_in, n_out, n_scratch = len(args), len(outs), len(scratch)

    def body(*refs):
        refs = list(refs)
        ins, results = refs[:n_in], refs[n_in : n_in + n_out]
        rest = refs[n_in + n_out :]
        own, rest = rest[:n_scratch], rest[n_scratch:]
        buffers, rest = rest[: len(staged)], rest[len(staged) :]
        out_buffers, rest = rest[: len(late)], rest[len(late) :]
        copies = {}
        for at, k in enumerate(staged):
            copies[k] = pltpu.make_async_copy(ins[k], buffers[at], rest[0].at[at])
            copies[k].start()
            ins[k] = buffers[at]
        targets = {}
        for at, k in enumerate(late):
            targets[k] = results[k]
            results[k] = out_buffers[at]

        def wait(*which):
            for k in which:
                copies.pop(k).wait()

        kernel(wait, *ins, *results, *own)
        assert not copies
        ends = [
            pltpu.make_async_copy(results[k], targets[k], rest[-1].at[at])
            for at, k in enumerate(late)
        ]
        for copy in ends:
            copy.start()
        for copy in ends:
            copy.wait()

    def like(x):
        return pltpu.VMEM(x.shape, x.dtype)

    extra = [like(args[k]) for k in staged] + [like(outs[k]) for k in late]
    extra += [pltpu.SemaphoreType.DMA((len(group),)) for group in (staged, late) if group]
    out_specs = tuple(pl.BlockSpec(memory_space=spaces[place]) for place in out_places)
    pinned = tuple(
        pltpu.HBM(x.shape, x.dtype) if place == "h" else x for x, place in zip(outs, out_places)
    )
    return pl.pallas_call(
        body,
        out_shape=pinned if several else pinned[0],
        in_specs=[pl.BlockSpec(memory_space=spaces[place]) for place in places],
        out_specs=out_specs if several else out_specs[0],
        scratch_shapes=list(scratch) + extra,
        compiler_params=pltpu.CompilerParams(vmem_limit_bytes=room << 20),
        cost_estimate=cost,
    )(*args)


def per_device(
    user_rows, user_row, segment, cand_feat, grad_score, u_weight, v_weight, bias, w_out
):
    user, feat, seg = user_rows[0], cand_feat[0], segment[0]
    peers, replicas = lax.axis_size("dp"), lax.axis_size("replica")
    req, width = user.shape
    rows = feat.shape[0]
    rank = u_weight.shape[1]
    part = width // peers
    piece = width // PIECES
    shape = jax.ShapeDtypeStruct
    bias, w_out = bias[None], w_out.reshape(width // LANES, LANES)
    pairs = [(i, i ^ 1) for i in range(replicas)]
    turn = round(TURN * peers)
    plane = [[(j + turn) % peers for j in range(peers)]]
    column = [[(j + replicas - 2) % replicas for j in range(replicas)]]
    message = (peers, PIECES, piece + LANES)
    slots, pack = call(
        request_kernel,
        (shape(message, BF16), shape((16 + req, width), BF16)),
        user_row, seg, grad_score, user, feat,
        places="hhhhp",
        scratch=[
            pltpu.VMEM(message, F32),
            pltpu.VMEM((rows, width), BF16),
            pltpu.SemaphoreType.DMA((PIECES,)),
        ],
    )
    arrived = lax.all_to_all(
        slots, "dp", split_axis=0, concat_axis=0, tiled=True, axis_index_groups=plane
    )
    swapped_feat = lax.ppermute(feat, "replica", pairs)
    swapped = lax.ppermute(pack, "replica", pairs)
    parts_shape = (peers, 8, 4 * rank + LANES)
    base, half, user_half, users = call(
        main_kernel,
        (
            shape(parts_shape, BF16),
            shape((width, rank), BF16),
            shape((2 * req, rank), F32),
            shape((2 * req, width), BF16),
        ),
        feat, swapped_feat, grad_score, user, swapped, w_out, u_weight, v_weight,
        places="pahhnhpp",
        out_places="h",
        scratch=[
            pltpu.VMEM((2 * rows, width), BF16),
            pltpu.VMEM((rank, width), BF16),
            pltpu.SemaphoreType.DMA((3,)),
        ],
        cost=pl.CostEstimate(flops=1, bytes_accessed=1, transcendentals=0),
    )
    own = call(
        pick_kernel,
        shape((req, width + LANES), BF16),
        arrived, user_half,
        places="-a",
        scratch=[pltpu.VMEM(message, F32)],
    )
    other = lax.ppermute(own, "replica", pairs)
    parts = call(
        merge_kernel,
        shape(parts_shape, BF16),
        own, other, users, half, user_half, base,
        places="-----h",
    )
    received = lax.all_to_all(
        parts, "dp", split_axis=0, concat_axis=0, tiled=True, axis_index_groups=plane
    )
    user_grad, tail = call(
        user_grad_kernel,
        (shape((req, width), F32), shape((part, rank + LANES), F32)),
        own, user, u_weight, v_weight, bias, w_out,
        places="-hhhhh",
    )
    copies = call(sum_kernel, shape((replicas, 8, 4 * rank + LANES), BF16), received)
    gathered = lax.all_to_all(
        copies, "replica", split_axis=0, concat_axis=0, tiled=True, axis_index_groups=column
    )
    factor = 1.0 / math.sqrt(rows * peers * replicas)
    grad_u, grad_vt, grad_bias, grad_out = call(
        functools.partial(last_kernel, factor),
        (
            shape((part, rank), F32),
            shape((part, rank), F32),
            shape((1, part), F32),
            shape((1, part), F32),
        ),
        gathered, tail,
        places="-n",
    )
    return (user_grad[None], grad_u, grad_vt, grad_bias[0], grad_out[0])


def solution(mesh):
    placed = (
        P("replica", "dp", None),
        P("replica", "dp"),
        P("replica", "dp", None),
        P("replica", "dp", None),
        P("replica", "dp"),
        P(),
        P(),
        P(),
        P(),
    )
    return jax.shard_map(
        per_device,
        mesh=mesh,
        in_specs=placed,
        out_specs=(P("replica", "dp", None), P("dp", None), P("dp", None), P("dp"), P("dp")),
        check_vma=False,
    )
```

```python
import functools
import math

import jax
import jax.numpy as jnp
from jax import lax
from jax.experimental import pallas as pl
from jax.experimental.pallas import tpu as pltpu
from jax.sharding import PartitionSpec as P

F32 = jnp.float32
BF16 = jnp.bfloat16
LANES = 128
PIECES = 2
TURN = 36 / 64
NT = (((1,), (1,)), ((), ()))
TN = (((0,), (0,)), ((), ()))


def dot(a, b, dims=(((1,), (0,)), ((), ()))):
    return lax.dot_general(a, b, dims, preferred_element_type=F32)


def iota(shape, dim):
    return lax.broadcasted_iota(jnp.int32, shape, dim)


def split_in_two(x):
    high = x.astype(BF16)
    return high, (x - high.astype(F32)).astype(BF16)


def as_columns(row):
    return jnp.transpose(jnp.broadcast_to(row, (LANES, row.shape[1])))


def request_kernel(
    wait, wanted_ref, seg_ref, score_ref, user_ref, feat_any, slots_ref, pack_ref, wide, feat_ref, sems
):
    peers, req = slots_ref.shape[0], wanted_ref.shape[1]
    rows, width = feat_ref.shape
    piece = width // PIECES
    parts = [pl.ds(p * piece, piece) for p in range(PIECES)]
    copies = [
        pltpu.make_async_copy(feat_any.at[:, part], feat_ref.at[:, part], sems.at[p])
        for p, part in enumerate(parts)
    ]
    for copy in copies:
        copy.start()
    wait(0, 1, 2)
    wanted = wanted_ref[...]
    owner = lax.div(wanted, jnp.int32(req))
    local = wanted - owner * req
    scores = score_ref[...]
    turn = round(TURN * peers)
    to_owner = (iota((peers, req), 0) == lax.rem(owner + (peers - turn), peers)).astype(BF16)
    place = (iota((LANES, req), 0) == local).astype(BF16)
    mine = iota((req, rows), 0) == seg_ref[...]
    total_high, total_low = split_in_two(
        jnp.sum(jnp.where(mine, scores, 0.0), axis=1, keepdims=True)
    )
    lane = iota((req, LANES), 1)
    totals = jnp.where(
        lane == req,
        total_high.astype(F32),
        jnp.where(lane == req + 1, total_low.astype(F32), 0.0),
    ).astype(BF16)
    extra = dot(to_owner, place, NT) + dot(to_owner, totals)
    weights = jnp.where(mine, scores, 0.0).astype(BF16)
    weights = dot(to_owner, weights).astype(BF16)
    wide[:, 0, piece:] = extra
    for p in range(1, PIECES):
        wide[:, p, piece:] = jnp.zeros((peers, LANES), F32)
    score_high, score_low = split_in_two(scores)
    line = iota((16, rows), 0)
    pack_ref[:16, :] = jnp.zeros((16, width), BF16)
    pack_ref[:16, :rows] = jnp.where(
        line == 0,
        score_high.astype(F32),
        jnp.where(line == 1, score_low.astype(F32), 0.0),
    ).astype(BF16)
    wait(3)
    pack_ref[16:, :] = user_ref[...]
    for p in range(PIECES):
        copies[p].wait()
        wide[:, p, :piece] = dot(weights, feat_ref[:, p * piece : (p + 1) * piece])
    slots_ref[...] = wide[...].astype(BF16)


def lay_out(grad, first, out_ref, base_ref=None):
    peers, rank = out_ref.shape[0], grad.shape[1]
    chunks = grad.shape[0] // 32
    at = (first - round(TURN * peers)) % peers
    blocks = grad.reshape(chunks, 4, 8, rank)
    written, done = [], 0
    while done < chunks:
        count = min(chunks - done, peers - at)
        place = slice(at, at + count)
        for q in range(4):
            part = slice(q * rank, (q + 1) * rank)
            block = blocks[done : done + count, q]
            if base_ref is not None:
                block = block + base_ref[place, :, part].astype(F32)
            out_ref[place, :, part] = block.astype(BF16)
        written.append(place)
        done, at = done + count, (at + count) % peers
    return written


def lay_sums(sums, out_ref):
    peers = out_ref.shape[0]
    part = sums.shape[1] // peers
    turn = round(TURN * peers)
    each = LANES // part
    turned = [sums] + [
        jnp.concatenate([sums[:, k * part :], sums[:, : k * part]], axis=1) for k in range(1, each)
    ]
    order = [(j + turn) % peers for j in range(peers)]
    lines = [
        turned[j % each][:, j // each * LANES : (j // each + 1) * LANES] for j in order
    ]
    lines = jnp.concatenate([jnp.broadcast_to(line, (8, LANES)) for line in lines], axis=0)
    out_ref[:, :, out_ref.shape[2] - LANES :] = lines.reshape(peers, 8, LANES).astype(BF16)


def row_of(ref):
    rows = ref[...].astype(F32)
    return jnp.concatenate([rows[k : k + 1, :] for k in range(rows.shape[0])], axis=1)


def my_core():
    return lax.rem(lax.axis_index("replica"), 2)


def main_kernel(
    wait, feat_any, other_any, score_ref, user_ref, pack_ref, w_ref, u_any, v_any,
    base_hbm, half_ref, user_half_ref, users_ref, both, v_ref, base_ref, sems,
):
    rows, width = feat_any.shape
    rank = v_ref.shape[0]
    req = user_ref.shape[0]
    peers = base_ref.shape[0]
    core = my_core()
    get_u = pltpu.make_async_copy(u_any, half_ref, sems.at[0])
    get_v = pltpu.make_async_copy(v_any, v_ref, sems.at[0])
    copies = [
        pltpu.make_async_copy(feat_any, both.at[:rows], sems.at[1]),
        pltpu.make_async_copy(other_any, both.at[rows:], sems.at[2]),
    ]
    pl.when(core == 0)(get_u.start)
    pl.when(core == 1)(get_v.start)
    for copy in copies:
        copy.start()
    wait(2, 3, 4, 5)
    users_ref[:req, :] = user_ref[...]
    users_ref[req:, :] = pack_ref[16:, :]
    marks = pack_ref[:16, :rows].astype(F32)
    scores = jnp.concatenate(
        [as_columns(score_ref[...]), as_columns(marks[0:1, :] + marks[1:2, :])], axis=0
    )
    pl.when(core == 0)(get_u.wait)

    @pl.when(core == 1)
    def _():
        get_v.wait()
        half_ref[...] = jnp.transpose((v_ref[...].astype(F32) * row_of(w_ref)).astype(BF16))

    half = half_ref[...]
    scaled = []
    for at, copy in zip((0, rows), copies):
        copy.wait()
        weight = scores[at : at + rows, :]
        low = dot(both[at : at + rows, :], half)
        scaled.append(
            jnp.concatenate(
                [low[:, k : k + LANES] * weight for k in range(0, rank, LANES)], axis=1
            ).astype(BF16)
        )
    scaled = jnp.concatenate(scaled, axis=0)
    ends = []
    for k in range(2):
        at = k * (width // 2)
        grad = dot(both[:, at : at + width // 2], scaled, TN)
        for place in lay_out(grad, k * (peers // 2), base_ref):
            ends.append(
                pltpu.make_async_copy(
                    base_ref.at[place], base_hbm.at[place], sems.at[3 + len(ends)]
                )
            )
            ends[-1].start()
    user_half_ref[...] = dot(users_ref[...], half)
    for copy in ends:
        copy.wait()


def pick_kernel(wait, slots_ref, after_any, out_ref, wide):
    req = out_ref.shape[0]
    piece = slots_ref.shape[2] - LANES
    wide[...] = slots_ref[...].astype(F32)
    extra = wide[:, 0, piece:].astype(BF16)
    lane = iota(extra.shape, 1)
    order = jnp.where(lane < req, extra.astype(F32), 0.0).astype(BF16)[:, :req]
    for p in range(PIECES):
        got = wide[:, p, :piece].astype(BF16)
        out_ref[:, p * piece : (p + 1) * piece] = dot(order, got, TN).astype(BF16)
    out_ref[:, PIECES * piece :] = dot(order, extra, TN).astype(BF16)


def total_of(pack, width, req):
    at = width + req
    return pack[:, at : at + 1].astype(F32) + pack[:, at + 1 : at + 2].astype(F32)


def merge_kernel(wait, own_ref, other_ref, users_ref, half_ref, user_half_ref, base_ref, out_ref):
    req, width = users_ref.shape[0] // 2, users_ref.shape[1]
    own, other = own_ref[...], other_ref[...]
    sums = jnp.concatenate([own[:, :width], other[:, :width]], axis=0)
    total = jnp.concatenate([total_of(own, width, req), total_of(other, width, req)], axis=0)
    users, user_half = users_ref[...], user_half_ref[...]
    both = dot(sums, half_ref[...]) + total * user_half
    grad = dot(
        jnp.concatenate([sums, users], axis=0),
        jnp.concatenate([user_half, both], axis=0).astype(BF16),
        TN,
    )
    lay_sums(
        jnp.sum(sums.astype(F32) + total * users.astype(F32), axis=0, keepdims=True), out_ref
    )
    wait(5)
    lay_out(grad, 0, out_ref, base_ref)


def user_grad_kernel(wait, pack_ref, user_ref, u_ref, v_ref, bias_ref, w_ref, out_ref, tail_ref):
    wait(*range(1, 6))
    req, width = user_ref.shape
    part, rank = tail_ref.shape[0], v_ref.shape[0]
    pack = pack_ref[...]
    sums = pack[:, :width]
    total = total_of(pack, width, req)
    user = user_ref[...]
    u, v = u_ref[...], v_ref[...]
    w_row = row_of(w_ref)
    low = dot(sums, u) + total * dot(user, u)
    both = (jnp.concatenate([sums, user], axis=0).astype(F32) * w_row).astype(BF16)
    both = dot(both, v, NT)
    grad_low = both[:req, :] + total * both[req:, :]
    out_ref[...] = (
        w_row * (dot(low.astype(BF16), v) + total * (bias_ref[...] + 1.0))
        + dot(grad_low.astype(BF16), u, NT)
    )
    here = iota((part, width), 1) == lax.axis_index("dp") * part + iota((part, width), 0)
    tail_ref[:, :rank] = dot(here.astype(BF16), v, NT)
    lane = iota((part, LANES), 1)
    w_col = jnp.sum(jnp.where(here, w_row, 0.0), axis=1, keepdims=True)
    b_col = jnp.sum(jnp.where(here, bias_ref[...], 0.0), axis=1, keepdims=True)
    tail_ref[:, rank:] = jnp.where(lane == 0, w_col, jnp.where(lane == 1, b_col, 0.0))


def sum_kernel(wait, in_ref, out_ref):
    total = jnp.sum(in_ref[...].astype(F32), axis=0).astype(BF16)
    out_ref[...] = jnp.broadcast_to(total[None], out_ref.shape)


def last_kernel(factor, wait, in_ref, tail_ref, grad_u_ref, grad_vt_ref, bias_ref, out_ref):
    wait(1)
    part, rank = grad_u_ref.shape
    replicas = in_ref.shape[0]
    sums = [
        sum(in_ref[k].astype(F32) for k in range(core, replicas, 2)) * factor for core in (0, 1)
    ]
    low, grad_low = (
        jnp.concatenate([s[:, q * rank : (q + 1) * rank] for q in range(4)], axis=0) for s in sums
    )
    column = as_columns(sums[0][0:1, 4 * rank :])[:part, 0:1]
    tail = tail_ref[...]
    w_col, b_col = tail[:, rank : rank + 1], tail[:, rank + 1 : rank + 2]
    grad_u_ref[...] = grad_low
    grad_vt_ref[...] = w_col * low
    out_col = jnp.sum(tail[:, :rank] * low, axis=1, keepdims=True) + (b_col + 1.0) * column
    bias_ref[...] = jnp.transpose(jnp.broadcast_to(w_col * column, (part, LANES)))[0:1, :]
    out_ref[...] = jnp.transpose(jnp.broadcast_to(out_col, (part, LANES)))[0:1, :]


def call(kernel, out, *args, places="", out_places="", scratch=(), room=24, cost=None):
    spaces = {"s": pltpu.SMEM, "a": pl.ANY, "h": pltpu.HBM, "n": pl.ANY, "p": pltpu.HBM, "-": pltpu.VMEM}
    several = isinstance(out, tuple)
    outs = out if several else (out,)
    places = places + "-" * (len(args) - len(places))
    out_places = out_places + "-" * (len(outs) - len(out_places))
    staged = [k for k, place in enumerate(places) if place in "hn"]
    late = [k for k, place in enumerate(out_places) if place in "hn"]
    args = [
        pltpu.with_memory_space_constraint(arg, pltpu.HBM) if place in "hp" else arg
        for arg, place in zip(args, places)
    ]
    n_in, n_out, n_scratch = len(args), len(outs), len(scratch)

    def body(*refs):
        refs = list(refs)
        ins, results = refs[:n_in], refs[n_in : n_in + n_out]
        rest = refs[n_in + n_out :]
        own, rest = rest[:n_scratch], rest[n_scratch:]
        buffers, rest = rest[: len(staged)], rest[len(staged) :]
        out_buffers, rest = rest[: len(late)], rest[len(late) :]
        copies = {}
        for at, k in enumerate(staged):
            copies[k] = pltpu.make_async_copy(ins[k], buffers[at], rest[0].at[at])
            copies[k].start()
            ins[k] = buffers[at]
        targets = {}
        for at, k in enumerate(late):
            targets[k] = results[k]
            results[k] = out_buffers[at]

        def wait(*which):
            for k in which:
                copies.pop(k).wait()

        kernel(wait, *ins, *results, *own)
        assert not copies
        ends = [
            pltpu.make_async_copy(results[k], targets[k], rest[-1].at[at])
            for at, k in enumerate(late)
        ]
        for copy in ends:
            copy.start()
        for copy in ends:
            copy.wait()

    def like(x):
        return pltpu.VMEM(x.shape, x.dtype)

    extra = [like(args[k]) for k in staged] + [like(outs[k]) for k in late]
    extra += [pltpu.SemaphoreType.DMA((len(group),)) for group in (staged, late) if group]
    out_specs = tuple(pl.BlockSpec(memory_space=spaces[place]) for place in out_places)
    pinned = tuple(
        pltpu.HBM(x.shape, x.dtype) if place in "hp" else x for x, place in zip(outs, out_places)
    )
    return pl.pallas_call(
        body,
        out_shape=pinned if several else pinned[0],
        in_specs=[pl.BlockSpec(memory_space=spaces[place]) for place in places],
        out_specs=out_specs if several else out_specs[0],
        scratch_shapes=list(scratch) + extra,
        compiler_params=pltpu.CompilerParams(vmem_limit_bytes=room << 20),
        cost_estimate=cost,
    )(*args)


def per_device(
    user_rows, user_row, segment, cand_feat, grad_score, u_weight, v_weight, bias, w_out
):
    user, feat, seg = user_rows[0], cand_feat[0], segment[0]
    peers, replicas = lax.axis_size("dp"), lax.axis_size("replica")
    req, width = user.shape
    rows = feat.shape[0]
    rank = u_weight.shape[1]
    part = width // peers
    piece = width // PIECES
    shape = jax.ShapeDtypeStruct
    bias, w_out = bias[None], w_out.reshape(width // LANES, LANES)
    pairs = [(i, i ^ 1) for i in range(replicas)]
    turn = round(TURN * peers)
    plane = [[(j + turn) % peers for j in range(peers)]]
    column = [[(j + replicas - 2) % replicas for j in range(replicas)]]
    message = (peers, PIECES, piece + LANES)
    slots, pack = call(
        request_kernel,
        (shape(message, BF16), shape((16 + req, width), BF16)),
        user_row, seg, grad_score, user, feat,
        places="hhhhp",
        scratch=[
            pltpu.VMEM(message, F32),
            pltpu.VMEM((rows, width), BF16),
            pltpu.SemaphoreType.DMA((PIECES,)),
        ],
    )
    arrived = lax.all_to_all(
        slots, "dp", split_axis=0, concat_axis=0, tiled=True, axis_index_groups=plane
    )
    swapped_feat = lax.ppermute(feat, "replica", pairs)
    swapped = lax.ppermute(pack, "replica", pairs)
    parts_shape = (peers, 8, 4 * rank + LANES)
    base, half, user_half, users = call(
        main_kernel,
        (
            shape((peers, 8, 4 * rank), BF16),
            shape((width, rank), BF16),
            shape((2 * req, rank), F32),
            shape((2 * req, width), BF16),
        ),
        feat, swapped_feat, grad_score, user, swapped, w_out, u_weight, v_weight,
        places="pahhnhpp",
        out_places="p",
        scratch=[
            pltpu.VMEM((2 * rows, width), BF16),
            pltpu.VMEM((rank, width), BF16),
            pltpu.VMEM((peers, 8, 4 * rank), BF16),
            pltpu.SemaphoreType.DMA((6,)),
        ],
        cost=pl.CostEstimate(flops=1, bytes_accessed=1, transcendentals=0),
    )
    own = call(
        pick_kernel,
        shape((req, width + LANES), BF16),
        arrived, user_half,
        places="-a",
        scratch=[pltpu.VMEM(message, F32)],
    )
    other = lax.ppermute(own, "replica", pairs)
    parts = call(
        merge_kernel,
        shape(parts_shape, BF16),
        own, other, users, half, user_half, base,
        places="-----h",
    )
    received = lax.all_to_all(
        parts, "dp", split_axis=0, concat_axis=0, tiled=True, axis_index_groups=plane
    )
    user_grad, tail = call(
        user_grad_kernel,
        (shape((req, width), F32), shape((part, rank + LANES), F32)),
        own, user, u_weight, v_weight, bias, w_out,
        places="-hhhhh",
    )
    copies = call(sum_kernel, shape((replicas, 8, 4 * rank + LANES), BF16), received)
    gathered = lax.all_to_all(
        copies, "replica", split_axis=0, concat_axis=0, tiled=True, axis_index_groups=column
    )
    factor = 1.0 / math.sqrt(rows * peers * replicas)
    grad_u, grad_vt, grad_bias, grad_out = call(
        functools.partial(last_kernel, factor),
        (
            shape((part, rank), F32),
            shape((part, rank), F32),
            shape((1, part), F32),
            shape((1, part), F32),
        ),
        gathered, tail,
        places="-n",
    )
    return (user_grad[None], grad_u, grad_vt, grad_bias[0], grad_out[0])


def solution(mesh):
    placed = (
        P("replica", "dp", None),
        P("replica", "dp"),
        P("replica", "dp", None),
        P("replica", "dp", None),
        P("replica", "dp"),
        P(),
        P(),
        P(),
        P(),
    )
    return jax.shard_map(
        per_device,
        mesh=mesh,
        in_specs=placed,
        out_specs=(P("replica", "dp", None), P("dp", None), P("dp", None), P("dp"), P("dp")),
        check_vma=False,
    )
```

```python
import functools
import math

import jax
import jax.numpy as jnp
from jax import lax
from jax.experimental import pallas as pl
from jax.experimental.pallas import tpu as pltpu
from jax.sharding import PartitionSpec as P

F32 = jnp.float32
BF16 = jnp.bfloat16
LANES = 128
PIECES = 2
TURN = 36 / 64
NT = (((1,), (1,)), ((), ()))
TN = (((0,), (0,)), ((), ()))


def dot(a, b, dims=(((1,), (0,)), ((), ()))):
    return lax.dot_general(a, b, dims, preferred_element_type=F32)


def iota(shape, dim):
    return lax.broadcasted_iota(jnp.int32, shape, dim)


def split_in_two(x):
    high = x.astype(BF16)
    return high, (x - high.astype(F32)).astype(BF16)


def as_columns(row):
    return jnp.transpose(jnp.broadcast_to(row, (LANES, row.shape[1])))


def request_kernel(
    wait, wanted_ref, seg_ref, score_ref, user_ref, feat_any, slots_ref, pack_ref, wide, feat_ref, sems
):
    peers, req = slots_ref.shape[0], wanted_ref.shape[1]
    rows, width = feat_ref.shape
    piece = width // PIECES
    parts = [pl.ds(p * piece, piece) for p in range(PIECES)]
    copies = [
        pltpu.make_async_copy(feat_any.at[:, part], feat_ref.at[:, part], sems.at[p])
        for p, part in enumerate(parts)
    ]
    for copy in copies:
        copy.start()
    wait(0, 1, 2)
    wanted = wanted_ref[...]
    assert req & (req - 1) == 0
    local = wanted & (req - 1)
    scores = score_ref[...]
    turn = round(TURN * peers)
    line = iota((peers, req), 0)
    first = jnp.where(line < peers - turn, line + turn, line + (turn - peers)) * req
    to_owner = (wanted - local == first).astype(BF16)
    place = (iota((LANES, req), 0) == local).astype(BF16)
    mine = iota((req, rows), 0) == seg_ref[...]
    total_high, total_low = split_in_two(
        jnp.sum(jnp.where(mine, scores, 0.0), axis=1, keepdims=True)
    )
    lane = iota((req, LANES), 1)
    totals = jnp.where(
        lane == req,
        total_high.astype(F32),
        jnp.where(lane == req + 1, total_low.astype(F32), 0.0),
    ).astype(BF16)
    extra = dot(to_owner, place, NT) + dot(to_owner, totals)
    weights = jnp.where(mine, scores, 0.0).astype(BF16)
    weights = dot(to_owner, weights).astype(BF16)
    wide[:, 0, piece:] = extra
    for p in range(1, PIECES):
        wide[:, p, piece:] = jnp.zeros((peers, LANES), F32)
    score_high, score_low = split_in_two(scores)
    line = iota((16, rows), 0)
    pack_ref[:16, :] = jnp.zeros((16, width), BF16)
    pack_ref[:16, :rows] = jnp.where(
        line == 0,
        score_high.astype(F32),
        jnp.where(line == 1, score_low.astype(F32), 0.0),
    ).astype(BF16)
    wait(3)
    pack_ref[16:, :] = user_ref[...]
    for p in range(PIECES):
        copies[p].wait()
        wide[:, p, :piece] = dot(weights, feat_ref[:, p * piece : (p + 1) * piece])
    slots_ref[...] = wide[...].astype(BF16)


def lay_out(grad, first, out_ref, base_ref=None):
    peers, rank = out_ref.shape[0], grad.shape[1]
    chunks = grad.shape[0] // 32
    at = (first - round(TURN * peers)) % peers
    blocks = grad.reshape(chunks, 4, 8, rank)
    written, done = [], 0
    while done < chunks:
        count = min(chunks - done, peers - at)
        place = slice(at, at + count)
        for q in range(4):
            part = slice(q * rank, (q + 1) * rank)
            block = blocks[done : done + count, q]
            if base_ref is not None:
                block = block + base_ref[place, :, part].astype(F32)
            out_ref[place, :, part] = block.astype(BF16)
        written.append(place)
        done, at = done + count, (at + count) % peers
    return written


def lay_sums(sums, out_ref):
    peers = out_ref.shape[0]
    part = sums.shape[1] // peers
    turn = round(TURN * peers)
    each = LANES // part
    turned = [sums] + [
        jnp.concatenate([sums[:, k * part :], sums[:, : k * part]], axis=1) for k in range(1, each)
    ]
    order = [(j + turn) % peers for j in range(peers)]
    lines = [
        turned[j % each][:, j // each * LANES : (j // each + 1) * LANES] for j in order
    ]
    lines = jnp.concatenate([jnp.broadcast_to(line, (8, LANES)) for line in lines], axis=0)
    out_ref[:, :, out_ref.shape[2] - LANES :] = lines.reshape(peers, 8, LANES).astype(BF16)


def row_of(ref):
    rows = ref[...].astype(F32)
    return jnp.concatenate([rows[k : k + 1, :] for k in range(rows.shape[0])], axis=1)


def my_core():
    return lax.rem(lax.axis_index("replica"), 2)


def main_kernel(
    wait, feat_any, other_any, score_ref, user_ref, pack_ref, w_ref, u_any, v_any,
    base_hbm, half_ref, user_half_ref, users_ref, both, v_ref, base_ref, sems,
):
    rows, width = feat_any.shape
    rank = v_ref.shape[0]
    req = user_ref.shape[0]
    peers = base_ref.shape[0]
    core = my_core()
    get_u = pltpu.make_async_copy(u_any, half_ref, sems.at[0])
    get_v = pltpu.make_async_copy(v_any, v_ref, sems.at[0])
    copies = [
        pltpu.make_async_copy(feat_any, both.at[:rows], sems.at[1]),
        pltpu.make_async_copy(other_any, both.at[rows:], sems.at[2]),
    ]
    pl.when(core == 0)(get_u.start)
    pl.when(core == 1)(get_v.start)
    for copy in copies:
        copy.start()
    wait(2, 3, 4, 5)
    users_ref[:req, :] = user_ref[...]
    users_ref[req:, :] = pack_ref[16:, :]
    marks = pack_ref[:16, :rows].astype(F32)
    scores = jnp.concatenate(
        [as_columns(score_ref[...]), as_columns(marks[0:1, :] + marks[1:2, :])], axis=0
    )
    pl.when(core == 0)(get_u.wait)

    @pl.when(core == 1)
    def _():
        get_v.wait()
        half_ref[...] = jnp.transpose((v_ref[...].astype(F32) * row_of(w_ref)).astype(BF16))

    half = half_ref[...]
    scaled = []
    for at, copy in zip((0, rows), copies):
        copy.wait()
        weight = scores[at : at + rows, :]
        low = dot(both[at : at + rows, :], half)
        scaled.append(
            jnp.concatenate(
                [low[:, k : k + LANES] * weight for k in range(0, rank, LANES)], axis=1
            ).astype(BF16)
        )
    scaled = jnp.concatenate(scaled, axis=0)
    ends = []
    for k in range(2):
        at = k * (width // 2)
        grad = dot(both[:, at : at + width // 2], scaled, TN)
        for place in lay_out(grad, k * (peers // 2), base_ref):
            ends.append(
                pltpu.make_async_copy(
                    base_ref.at[place], base_hbm.at[place], sems.at[3 + len(ends)]
                )
            )
            ends[-1].start()
    user_half_ref[...] = dot(users_ref[...], half)
    for copy in ends:
        copy.wait()


def pick_kernel(wait, slots_ref, after_any, out_ref, wide):
    req = out_ref.shape[0]
    piece = slots_ref.shape[2] - LANES
    wide[...] = slots_ref[...].astype(F32)
    extra = wide[:, 0, piece:].astype(BF16)
    lane = iota(extra.shape, 1)
    order = jnp.where(lane < req, extra.astype(F32), 0.0).astype(BF16)[:, :req]
    for p in range(PIECES):
        got = wide[:, p, :piece].astype(BF16)
        out_ref[:, p * piece : (p + 1) * piece] = dot(order, got, TN).astype(BF16)
    out_ref[:, PIECES * piece :] = dot(order, extra, TN).astype(BF16)


def total_of(pack, width, req):
    at = width + req
    return pack[:, at : at + 1].astype(F32) + pack[:, at + 1 : at + 2].astype(F32)


def merge_kernel(wait, own_ref, other_ref, users_ref, half_ref, user_half_ref, base_ref, out_ref):
    req, width = users_ref.shape[0] // 2, users_ref.shape[1]
    own, other = own_ref[...], other_ref[...]
    sums = jnp.concatenate([own[:, :width], other[:, :width]], axis=0)
    total = jnp.concatenate([total_of(own, width, req), total_of(other, width, req)], axis=0)
    users, user_half = users_ref[...], user_half_ref[...]
    both = dot(sums, half_ref[...]) + total * user_half
    grad = dot(
        jnp.concatenate([sums, users], axis=0),
        jnp.concatenate([user_half, both], axis=0).astype(BF16),
        TN,
    )
    lay_sums(
        jnp.sum(sums.astype(F32) + total * users.astype(F32), axis=0, keepdims=True), out_ref
    )
    wait(5)
    lay_out(grad, 0, out_ref, base_ref)


def user_grad_kernel(wait, pack_ref, user_ref, u_ref, v_ref, bias_ref, w_ref, out_ref, tail_ref):
    wait(*range(1, 6))
    req, width = user_ref.shape
    part, rank = tail_ref.shape[0], v_ref.shape[0]
    pack = pack_ref[...]
    sums = pack[:, :width]
    total = total_of(pack, width, req)
    user = user_ref[...]
    u, v = u_ref[...], v_ref[...]
    w_row = row_of(w_ref)
    low = dot(sums, u) + total * dot(user, u)
    both = (jnp.concatenate([sums, user], axis=0).astype(F32) * w_row).astype(BF16)
    both = dot(both, v, NT)
    grad_low = both[:req, :] + total * both[req:, :]
    out_ref[...] = (
        w_row * (dot(low.astype(BF16), v) + total * (bias_ref[...] + 1.0))
        + dot(grad_low.astype(BF16), u, NT)
    )
    here = iota((part, width), 1) == lax.axis_index("dp") * part + iota((part, width), 0)
    tail_ref[:, :rank] = dot(here.astype(BF16), v, NT)
    lane = iota((part, LANES), 1)
    w_col = jnp.sum(jnp.where(here, w_row, 0.0), axis=1, keepdims=True)
    b_col = jnp.sum(jnp.where(here, bias_ref[...], 0.0), axis=1, keepdims=True)
    tail_ref[:, rank:] = jnp.where(lane == 0, w_col, jnp.where(lane == 1, b_col, 0.0))


def sum_kernel(wait, in_ref, out_ref):
    total = jnp.sum(in_ref[...].astype(F32), axis=0).astype(BF16)
    out_ref[...] = jnp.broadcast_to(total[None], out_ref.shape)


def last_kernel(factor, wait, in_ref, tail_ref, grad_u_ref, grad_vt_ref, bias_ref, out_ref):
    wait(1)
    part, rank = grad_u_ref.shape
    replicas = in_ref.shape[0]
    sums = [
        sum(in_ref[k].astype(F32) for k in range(1 - core, replicas, 2)) * factor
        for core in (0, 1)
    ]
    low, grad_low = (
        jnp.concatenate([s[:, q * rank : (q + 1) * rank] for q in range(4)], axis=0) for s in sums
    )
    column = as_columns(sums[0][0:1, 4 * rank :])[:part, 0:1]
    tail = tail_ref[...]
    w_col, b_col = tail[:, rank : rank + 1], tail[:, rank + 1 : rank + 2]
    grad_u_ref[...] = grad_low
    grad_vt_ref[...] = w_col * low
    out_col = jnp.sum(tail[:, :rank] * low, axis=1, keepdims=True) + (b_col + 1.0) * column
    bias_ref[...] = jnp.transpose(jnp.broadcast_to(w_col * column, (part, LANES)))[0:1, :]
    out_ref[...] = jnp.transpose(jnp.broadcast_to(out_col, (part, LANES)))[0:1, :]


def call(kernel, out, *args, places="", out_places="", scratch=(), room=24, cost=None):
    spaces = {"s": pltpu.SMEM, "a": pl.ANY, "h": pltpu.HBM, "n": pl.ANY, "p": pltpu.HBM, "-": pltpu.VMEM}
    several = isinstance(out, tuple)
    outs = out if several else (out,)
    places = places + "-" * (len(args) - len(places))
    out_places = out_places + "-" * (len(outs) - len(out_places))
    staged = [k for k, place in enumerate(places) if place in "hn"]
    late = [k for k, place in enumerate(out_places) if place in "hn"]
    args = [
        pltpu.with_memory_space_constraint(arg, pltpu.HBM) if place in "hp" else arg
        for arg, place in zip(args, places)
    ]
    n_in, n_out, n_scratch = len(args), len(outs), len(scratch)

    def body(*refs):
        refs = list(refs)
        ins, results = refs[:n_in], refs[n_in : n_in + n_out]
        rest = refs[n_in + n_out :]
        own, rest = rest[:n_scratch], rest[n_scratch:]
        buffers, rest = rest[: len(staged)], rest[len(staged) :]
        out_buffers, rest = rest[: len(late)], rest[len(late) :]
        copies = {}
        for at, k in enumerate(staged):
            copies[k] = pltpu.make_async_copy(ins[k], buffers[at], rest[0].at[at])
            copies[k].start()
            ins[k] = buffers[at]
        targets = {}
        for at, k in enumerate(late):
            targets[k] = results[k]
            results[k] = out_buffers[at]

        def wait(*which):
            for k in which:
                copies.pop(k).wait()

        kernel(wait, *ins, *results, *own)
        assert not copies
        ends = [
            pltpu.make_async_copy(results[k], targets[k], rest[-1].at[at])
            for at, k in enumerate(late)
        ]
        for copy in ends:
            copy.start()
        for copy in ends:
            copy.wait()

    def like(x):
        return pltpu.VMEM(x.shape, x.dtype)

    extra = [like(args[k]) for k in staged] + [like(outs[k]) for k in late]
    extra += [pltpu.SemaphoreType.DMA((len(group),)) for group in (staged, late) if group]
    out_specs = tuple(pl.BlockSpec(memory_space=spaces[place]) for place in out_places)
    pinned = tuple(
        pltpu.HBM(x.shape, x.dtype) if place in "hp" else x for x, place in zip(outs, out_places)
    )
    return pl.pallas_call(
        body,
        out_shape=pinned if several else pinned[0],
        in_specs=[pl.BlockSpec(memory_space=spaces[place]) for place in places],
        out_specs=out_specs if several else out_specs[0],
        scratch_shapes=list(scratch) + extra,
        compiler_params=pltpu.CompilerParams(vmem_limit_bytes=room << 20),
        cost_estimate=cost,
    )(*args)


def per_device(
    user_rows, user_row, segment, cand_feat, grad_score, u_weight, v_weight, bias, w_out
):
    user, feat, seg = user_rows[0], cand_feat[0], segment[0]
    peers, replicas = lax.axis_size("dp"), lax.axis_size("replica")
    req, width = user.shape
    rows = feat.shape[0]
    rank = u_weight.shape[1]
    part = width // peers
    piece = width // PIECES
    shape = jax.ShapeDtypeStruct
    bias, w_out = bias[None], w_out.reshape(width // LANES, LANES)
    pairs = [(i, i ^ 1) for i in range(replicas)]
    turn = round(TURN * peers)
    plane = [[(j + turn) % peers for j in range(peers)]]
    column = [[((j ^ 1) + replicas - 2) % replicas for j in range(replicas)]]
    message = (peers, PIECES, piece + LANES)
    slots, pack = call(
        request_kernel,
        (shape(message, BF16), shape((16 + req, width), BF16)),
        user_row, seg, grad_score, user, feat,
        places="hhhhp",
        scratch=[
            pltpu.VMEM(message, F32),
            pltpu.VMEM((rows, width), BF16),
            pltpu.SemaphoreType.DMA((PIECES,)),
        ],
    )
    arrived = lax.all_to_all(
        slots, "dp", split_axis=0, concat_axis=0, tiled=True, axis_index_groups=plane
    )
    swapped_feat = lax.ppermute(feat, "replica", pairs)
    swapped = lax.ppermute(pack, "replica", pairs)
    parts_shape = (peers, 8, 4 * rank + LANES)
    base, half, user_half, users = call(
        main_kernel,
        (
            shape((peers, 8, 4 * rank), BF16),
            shape((width, rank), BF16),
            shape((2 * req, rank), F32),
            shape((2 * req, width), BF16),
        ),
        feat, swapped_feat, grad_score, user, swapped, w_out, u_weight, v_weight,
        places="pahhnhpp",
        out_places="p",
        scratch=[
            pltpu.VMEM((2 * rows, width), BF16),
            pltpu.VMEM((rank, width), BF16),
            pltpu.VMEM((peers, 8, 4 * rank), BF16),
            pltpu.SemaphoreType.DMA((6,)),
        ],
        cost=pl.CostEstimate(flops=1, bytes_accessed=1, transcendentals=0),
    )
    own = call(
        pick_kernel,
        shape((req, width + LANES), BF16),
        arrived, user_half,
        places="-a",
        scratch=[pltpu.VMEM(message, F32)],
    )
    other = lax.ppermute(own, "replica", pairs)
    parts = call(
        merge_kernel,
        shape(parts_shape, BF16),
        own, other, users, half, user_half, base,
        places="-----h",
    )
    received = lax.all_to_all(
        parts, "dp", split_axis=0, concat_axis=0, tiled=True, axis_index_groups=plane
    )
    user_grad, tail = call(
        user_grad_kernel,
        (shape((req, width), F32), shape((part, rank + LANES), F32)),
        own, user, u_weight, v_weight, bias, w_out,
        places="-hhhhh",
    )
    copies = call(sum_kernel, shape((replicas, 8, 4 * rank + LANES), BF16), received)
    gathered = lax.all_to_all(
        copies, "replica", split_axis=0, concat_axis=0, tiled=True, axis_index_groups=column
    )
    factor = 1.0 / math.sqrt(rows * peers * replicas)
    grad_u, grad_vt, grad_bias, grad_out = call(
        functools.partial(last_kernel, factor),
        (
            shape((part, rank), F32),
            shape((part, rank), F32),
            shape((1, part), F32),
            shape((1, part), F32),
        ),
        gathered, tail,
        places="-n",
    )
    return (user_grad[None], grad_u, grad_vt, grad_bias[0], grad_out[0])


def solution(mesh):
    placed = (
        P("replica", "dp", None),
        P("replica", "dp"),
        P("replica", "dp", None),
        P("replica", "dp", None),
        P("replica", "dp"),
        P(),
        P(),
        P(),
        P(),
    )
    return jax.shard_map(
        per_device,
        mesh=mesh,
        in_specs=placed,
        out_specs=(P("replica", "dp", None), P("dp", None), P("dp", None), P("dp"), P("dp")),
        check_vma=False,
    )
```

```python
import functools
import math

import jax
import jax.numpy as jnp
from jax import lax
from jax.experimental import pallas as pl
from jax.experimental.pallas import tpu as pltpu
from jax.sharding import PartitionSpec as P

F32 = jnp.float32
BF16 = jnp.bfloat16
LANES = 128
PIECES = 2
TURN = 36 / 64
NT = (((1,), (1,)), ((), ()))
TN = (((0,), (0,)), ((), ()))


def dot(a, b, dims=(((1,), (0,)), ((), ()))):
    return lax.dot_general(a, b, dims, preferred_element_type=F32)


def iota(shape, dim):
    return lax.broadcasted_iota(jnp.int32, shape, dim)


def split_in_two(x):
    high = x.astype(BF16)
    return high, (x - high.astype(F32)).astype(BF16)


def as_columns(row):
    return jnp.transpose(jnp.broadcast_to(row, (LANES, row.shape[1])))


def request_kernel(
    wait, wanted_ref, seg_ref, score_ref, user_ref, feat_any, slots_ref, pack_ref, wide, feat_ref, sems
):
    peers, req = slots_ref.shape[0], wanted_ref.shape[1]
    rows, width = feat_ref.shape
    piece = width // PIECES
    parts = [pl.ds(p * piece, piece) for p in range(PIECES)]
    copies = [
        pltpu.make_async_copy(feat_any.at[:, part], feat_ref.at[:, part], sems.at[p])
        for p, part in enumerate(parts)
    ]
    for copy in copies:
        copy.start()
    wait(0, 1, 2)
    wanted = wanted_ref[...]
    assert req & (req - 1) == 0
    local = wanted & (req - 1)
    scores = score_ref[...]
    turn = round(TURN * peers)
    line = iota((peers, req), 0)
    first = jnp.where(line < peers - turn, line + turn, line + (turn - peers)) * req
    to_owner = (wanted - local == first).astype(BF16)
    place = (iota((LANES, req), 0) == local).astype(BF16)
    mine = iota((req, rows), 0) == seg_ref[...]
    total_high, total_low = split_in_two(
        jnp.sum(jnp.where(mine, scores, 0.0), axis=1, keepdims=True)
    )
    lane = iota((req, LANES), 1)
    totals = jnp.where(
        lane == req,
        total_high.astype(F32),
        jnp.where(lane == req + 1, total_low.astype(F32), 0.0),
    ).astype(BF16)
    extra = dot(to_owner, place, NT) + dot(to_owner, totals)
    weights = jnp.where(mine, scores, 0.0).astype(BF16)
    weights = dot(to_owner, weights).astype(BF16)
    wide[:, 0, piece:] = extra
    for p in range(1, PIECES):
        wide[:, p, piece:] = jnp.zeros((peers, LANES), F32)
    score_high, score_low = split_in_two(scores)
    line = iota((16, rows), 0)
    pack_ref[:16, :] = jnp.zeros((16, width), BF16)
    pack_ref[:16, :rows] = jnp.where(
        line == 0,
        score_high.astype(F32),
        jnp.where(line == 1, score_low.astype(F32), 0.0),
    ).astype(BF16)
    wait(3)
    pack_ref[16:, :] = user_ref[...]
    for p in range(PIECES):
        copies[p].wait()
        wide[:, p, :piece] = dot(weights, feat_ref[:, p * piece : (p + 1) * piece])
    slots_ref[...] = wide[...].astype(BF16)


def lay_out(grad, first, out_ref, base_ref=None):
    peers, rank = out_ref.shape[0], grad.shape[1]
    chunks = grad.shape[0] // 32
    at = (first - round(TURN * peers)) % peers
    blocks = grad.reshape(chunks, 4, 8, rank)
    written, done = [], 0
    while done < chunks:
        count = min(chunks - done, peers - at)
        place = slice(at, at + count)
        for q in range(4):
            part = slice(q * rank, (q + 1) * rank)
            block = blocks[done : done + count, q]
            if base_ref is not None:
                block = block + base_ref[place, :, part].astype(F32)
            out_ref[place, :, part] = block.astype(BF16)
        written.append(place)
        done, at = done + count, (at + count) % peers
    return written


def lay_sums(sums, out_ref):
    peers = out_ref.shape[0]
    part = sums.shape[1] // peers
    turn = round(TURN * peers)
    each = LANES // part
    turned = [sums] + [
        jnp.concatenate([sums[:, k * part :], sums[:, : k * part]], axis=1) for k in range(1, each)
    ]
    order = [(j + turn) % peers for j in range(peers)]
    lines = [
        turned[j % each][:, j // each * LANES : (j // each + 1) * LANES] for j in order
    ]
    lines = jnp.concatenate([jnp.broadcast_to(line, (8, LANES)) for line in lines], axis=0)
    out_ref[:, :, out_ref.shape[2] - LANES :] = lines.reshape(peers, 8, LANES).astype(BF16)


def row_of(ref):
    rows = ref[...].astype(F32)
    return jnp.concatenate([rows[k : k + 1, :] for k in range(rows.shape[0])], axis=1)


def my_core():
    return lax.rem(lax.axis_index("replica"), 2)


def main_kernel(
    wait, feat_any, other_any, score_ref, user_ref, pack_ref, w_ref, u_any, v_any,
    base_hbm, half_ref, user_half_ref, users_ref, both, v_ref, base_ref, sems,
):
    rows, width = feat_any.shape
    rank = v_ref.shape[0]
    req = user_ref.shape[0]
    peers = base_ref.shape[0]
    core = my_core()
    get_u = pltpu.make_async_copy(u_any, half_ref, sems.at[0])
    get_v = pltpu.make_async_copy(v_any, v_ref, sems.at[0])
    copies = [
        pltpu.make_async_copy(feat_any, both.at[:rows], sems.at[1]),
        pltpu.make_async_copy(other_any, both.at[rows:], sems.at[2]),
    ]
    pl.when(core == 0)(get_u.start)
    pl.when(core == 1)(get_v.start)
    for copy in copies:
        copy.start()
    wait(2, 3, 4, 5)
    users_ref[:req, :] = user_ref[...]
    users_ref[req:, :] = pack_ref[16:, :]
    marks = pack_ref[:16, :rows].astype(F32)
    scores = jnp.concatenate(
        [as_columns(score_ref[...]), as_columns(marks[0:1, :] + marks[1:2, :])], axis=0
    )
    pl.when(core == 0)(get_u.wait)

    @pl.when(core == 1)
    def _():
        get_v.wait()
        half_ref[...] = jnp.transpose((v_ref[...].astype(F32) * row_of(w_ref)).astype(BF16))

    half = half_ref[...]
    scaled = []
    for at, copy in zip((0, rows), copies):
        copy.wait()
        weight = scores[at : at + rows, :]
        low = dot(both[at : at + rows, :], half)
        scaled.append(
            jnp.concatenate(
                [low[:, k : k + LANES] * weight for k in range(0, rank, LANES)], axis=1
            ).astype(BF16)
        )
    scaled = jnp.concatenate(scaled, axis=0)
    ends = []
    for k in range(2):
        at = k * (width // 2)
        grad = dot(both[:, at : at + width // 2], scaled, TN)
        for place in lay_out(grad, k * (peers // 2), base_ref):
            ends.append(
                pltpu.make_async_copy(
                    base_ref.at[place], base_hbm.at[place], sems.at[3 + len(ends)]
                )
            )
            ends[-1].start()
    user_half_ref[...] = dot(users_ref[...], half)
    for copy in ends:
        copy.wait()


def pick_kernel(wait, slots_ref, after_any, out_ref, wide):
    req = out_ref.shape[0]
    piece = slots_ref.shape[2] - LANES
    wide[...] = slots_ref[...].astype(F32)
    extra = wide[:, 0, piece:].astype(BF16)
    lane = iota(extra.shape, 1)
    order = jnp.where(lane < req, extra.astype(F32), 0.0).astype(BF16)[:, :req]
    for p in range(PIECES):
        got = wide[:, p, :piece].astype(BF16)
        out_ref[:, p * piece : (p + 1) * piece] = dot(order, got, TN).astype(BF16)
    out_ref[:, PIECES * piece :] = dot(order, extra, TN).astype(BF16)


def total_of(pack, width, req):
    at = width + req
    return pack[:, at : at + 1].astype(F32) + pack[:, at + 1 : at + 2].astype(F32)


def merge_kernel(wait, own_ref, other_ref, users_ref, half_ref, user_half_ref, base_ref, out_ref):
    req, width = users_ref.shape[0] // 2, users_ref.shape[1]
    own, other = own_ref[...], other_ref[...]
    sums = jnp.concatenate([own[:, :width], other[:, :width]], axis=0)
    total = jnp.concatenate([total_of(own, width, req), total_of(other, width, req)], axis=0)
    users, user_half = users_ref[...], user_half_ref[...]
    both = dot(sums, half_ref[...]) + total * user_half
    grad = dot(
        jnp.concatenate([sums, users], axis=0),
        jnp.concatenate([user_half, both], axis=0).astype(BF16),
        TN,
    )
    lay_sums(
        jnp.sum(sums.astype(F32) + total * users.astype(F32), axis=0, keepdims=True), out_ref
    )
    wait(5)
    lay_out(grad, 0, out_ref, base_ref)


def user_grad_kernel(wait, pack_ref, user_ref, u_ref, v_ref, bias_ref, w_ref, out_ref, tail_ref):
    wait(*range(1, 6))
    req, width = user_ref.shape
    part, rank = tail_ref.shape[0], v_ref.shape[0]
    pack = pack_ref[...]
    sums = pack[:, :width]
    total = total_of(pack, width, req)
    user = user_ref[...]
    u, v = u_ref[...], v_ref[...]
    w_row = row_of(w_ref)
    low = dot(sums, u) + total * dot(user, u)
    both = (jnp.concatenate([sums, user], axis=0).astype(F32) * w_row).astype(BF16)
    both = dot(both, v, NT)
    grad_low = both[:req, :] + total * both[req:, :]
    out_ref[...] = (
        w_row * (dot(low.astype(BF16), v) + total * (bias_ref[...] + 1.0))
        + dot(grad_low.astype(BF16), u, NT)
    )
    here = iota((part, width), 1) == lax.axis_index("dp") * part + iota((part, width), 0)
    tail_ref[:, :rank] = dot(here.astype(BF16), v, NT)
    lane = iota((part, LANES), 1)
    w_col = jnp.sum(jnp.where(here, w_row, 0.0), axis=1, keepdims=True)
    b_col = jnp.sum(jnp.where(here, bias_ref[...], 0.0), axis=1, keepdims=True)
    tail_ref[:, rank:] = jnp.where(lane == 0, w_col, jnp.where(lane == 1, b_col, 0.0))


def sum_kernel(wait, in_ref, out_ref):
    total = jnp.sum(in_ref[...].astype(F32), axis=0).astype(BF16)
    out_ref[...] = jnp.broadcast_to(total[None], out_ref.shape)


def last_kernel(factor, wait, in_ref, tail_ref, grad_u_ref, grad_vt_ref, bias_ref, out_ref):
    part, rank = grad_u_ref.shape
    replicas = in_ref.shape[0]
    sums = [
        sum(in_ref[k].astype(F32) for k in range(1 - core, replicas, 2)) * factor
        for core in (0, 1)
    ]
    low, grad_low = (
        jnp.concatenate([s[:, q * rank : (q + 1) * rank] for q in range(4)], axis=0) for s in sums
    )
    column = as_columns(sums[0][0:1, 4 * rank :])[:part, 0:1]
    tail = tail_ref[...]
    w_col, b_col = tail[:, rank : rank + 1], tail[:, rank + 1 : rank + 2]
    grad_u_ref[...] = grad_low
    grad_vt_ref[...] = w_col * low
    out_col = jnp.sum(tail[:, :rank] * low, axis=1, keepdims=True) + (b_col + 1.0) * column
    bias_ref[...] = jnp.transpose(jnp.broadcast_to(w_col * column, (part, LANES)))[0:1, :]
    out_ref[...] = jnp.transpose(jnp.broadcast_to(out_col, (part, LANES)))[0:1, :]


def call(kernel, out, *args, places="", out_places="", scratch=(), room=24, cost=None):
    spaces = {"s": pltpu.SMEM, "a": pl.ANY, "h": pltpu.HBM, "n": pl.ANY, "p": pltpu.HBM, "-": pltpu.VMEM}
    several = isinstance(out, tuple)
    outs = out if several else (out,)
    places = places + "-" * (len(args) - len(places))
    out_places = out_places + "-" * (len(outs) - len(out_places))
    staged = [k for k, place in enumerate(places) if place in "hn"]
    late = [k for k, place in enumerate(out_places) if place in "hn"]
    args = [
        pltpu.with_memory_space_constraint(arg, pltpu.HBM) if place in "hp" else arg
        for arg, place in zip(args, places)
    ]
    n_in, n_out, n_scratch = len(args), len(outs), len(scratch)

    def body(*refs):
        refs = list(refs)
        ins, results = refs[:n_in], refs[n_in : n_in + n_out]
        rest = refs[n_in + n_out :]
        own, rest = rest[:n_scratch], rest[n_scratch:]
        buffers, rest = rest[: len(staged)], rest[len(staged) :]
        out_buffers, rest = rest[: len(late)], rest[len(late) :]
        copies = {}
        for at, k in enumerate(staged):
            copies[k] = pltpu.make_async_copy(ins[k], buffers[at], rest[0].at[at])
            copies[k].start()
            ins[k] = buffers[at]
        targets = {}
        for at, k in enumerate(late):
            targets[k] = results[k]
            results[k] = out_buffers[at]

        def wait(*which):
            for k in which:
                copies.pop(k).wait()

        kernel(wait, *ins, *results, *own)
        assert not copies
        ends = [
            pltpu.make_async_copy(results[k], targets[k], rest[-1].at[at])
            for at, k in enumerate(late)
        ]
        for copy in ends:
            copy.start()
        for copy in ends:
            copy.wait()

    def like(x):
        return pltpu.VMEM(x.shape, x.dtype)

    extra = [like(args[k]) for k in staged] + [like(outs[k]) for k in late]
    extra += [pltpu.SemaphoreType.DMA((len(group),)) for group in (staged, late) if group]
    out_specs = tuple(pl.BlockSpec(memory_space=spaces[place]) for place in out_places)
    pinned = tuple(
        pltpu.HBM(x.shape, x.dtype) if place in "hp" else x for x, place in zip(outs, out_places)
    )
    return pl.pallas_call(
        body,
        out_shape=pinned if several else pinned[0],
        in_specs=[pl.BlockSpec(memory_space=spaces[place]) for place in places],
        out_specs=out_specs if several else out_specs[0],
        scratch_shapes=list(scratch) + extra,
        compiler_params=pltpu.CompilerParams(vmem_limit_bytes=room << 20),
        cost_estimate=cost,
    )(*args)


def per_device(
    user_rows, user_row, segment, cand_feat, grad_score, u_weight, v_weight, bias, w_out
):
    user, feat, seg = user_rows[0], cand_feat[0], segment[0]
    peers, replicas = lax.axis_size("dp"), lax.axis_size("replica")
    req, width = user.shape
    rows = feat.shape[0]
    rank = u_weight.shape[1]
    part = width // peers
    piece = width // PIECES
    shape = jax.ShapeDtypeStruct
    bias, w_out = bias[None], w_out.reshape(width // LANES, LANES)
    pairs = [(i, i ^ 1) for i in range(replicas)]
    turn = round(TURN * peers)
    plane = [[(j + turn) % peers for j in range(peers)]]
    column = [[((j ^ 1) + replicas - 2) % replicas for j in range(replicas)]]
    message = (peers, PIECES, piece + LANES)
    slots, pack = call(
        request_kernel,
        (shape(message, BF16), shape((16 + req, width), BF16)),
        user_row, seg, grad_score, user, feat,
        places="hhhhp",
        scratch=[
            pltpu.VMEM(message, F32),
            pltpu.VMEM((rows, width), BF16),
            pltpu.SemaphoreType.DMA((PIECES,)),
        ],
    )
    arrived = lax.all_to_all(
        slots, "dp", split_axis=0, concat_axis=0, tiled=True, axis_index_groups=plane
    )
    swapped_feat = lax.ppermute(feat, "replica", pairs)
    swapped = lax.ppermute(pack, "replica", pairs)
    parts_shape = (peers, 8, 4 * rank + LANES)
    base, half, user_half, users = call(
        main_kernel,
        (
            shape((peers, 8, 4 * rank), BF16),
            shape((width, rank), BF16),
            shape((2 * req, rank), F32),
            shape((2 * req, width), BF16),
        ),
        feat, swapped_feat, grad_score, user, swapped, w_out, u_weight, v_weight,
        places="pahhnhpp",
        out_places="p",
        scratch=[
            pltpu.VMEM((2 * rows, width), BF16),
            pltpu.VMEM((rank, width), BF16),
            pltpu.VMEM((peers, 8, 4 * rank), BF16),
            pltpu.SemaphoreType.DMA((6,)),
        ],
        cost=pl.CostEstimate(flops=1, bytes_accessed=1, transcendentals=0),
    )
    own = call(
        pick_kernel,
        shape((req, width + LANES), BF16),
        arrived, user_half,
        places="-a",
        scratch=[pltpu.VMEM(message, F32)],
    )
    other = lax.ppermute(own, "replica", pairs)
    parts = call(
        merge_kernel,
        shape(parts_shape, BF16),
        own, other, users, half, user_half, base,
        places="-----h",
    )
    received = lax.all_to_all(
        parts, "dp", split_axis=0, concat_axis=0, tiled=True, axis_index_groups=plane
    )
    user_grad, tail = call(
        user_grad_kernel,
        (shape((req, width), F32), shape((part, rank + LANES), F32)),
        own, user, u_weight, v_weight, bias, w_out,
        places="-hhhhh",
    )
    copies = call(sum_kernel, shape((replicas, 8, 4 * rank + LANES), BF16), received)
    gathered = lax.all_to_all(
        copies, "replica", split_axis=0, concat_axis=0, tiled=True, axis_index_groups=column
    )
    factor = 1.0 / math.sqrt(rows * peers * replicas)
    grad_u, grad_vt, grad_bias, grad_out = call(
        functools.partial(last_kernel, factor),
        (
            shape((part, rank), F32),
            shape((part, rank), F32),
            shape((1, part), F32),
            shape((1, part), F32),
        ),
        gathered, tail,
    )
    return (user_grad[None], grad_u, grad_vt, grad_bias[0], grad_out[0])


def solution(mesh):
    placed = (
        P("replica", "dp", None),
        P("replica", "dp"),
        P("replica", "dp", None),
        P("replica", "dp", None),
        P("replica", "dp"),
        P(),
        P(),
        P(),
        P(),
    )
    return jax.shard_map(
        per_device,
        mesh=mesh,
        in_specs=placed,
        out_specs=(P("replica", "dp", None), P("dp", None), P("dp", None), P("dp"), P("dp")),
        check_vma=False,
    )
```
